128 devices in a mesh: row: 8 (over y, core), col: 16 (over z, x).
Axes of the slice: x: 4, y: 4, z: 4, core: 2. Of those that a mesh axis runs over, the one named last changes fastest.
Arguments:
- inverse: float32 [16384, 16384], P('row', 'col'), may hold values from -6 to 6
- front_blocks: int32 [2, 32], replicated, may hold values from 0 to 63, as said below
- panels: float32 [2, 8192, 256], P(None, 'row'), may hold values from -0.0625 to 0.0625
- diag_terms: float32 [2, 256, 256], replicated, may hold values from -6 to 6
- bounds: int32 [2, 4], replicated, may hold values from 1 to 128, 256 in all within a row
Outputs:
- border: float32 [2, 8192, 256], P(None, ('row', 'col'))
- diag_block: float32 [2, 256, 256], replicated
The draws below stay inside these ranges and needn't reach their ends.
Inputs may be any that keep to these rules, and one draw needn't show every extreme that they name: `front_blocks`: each row names 32 distinct blocks. Positions 4 r to 4 r + 3 name blocks of four different groups of 8 consecutive blocks, and every such group is named at exactly four positions, of four different r. Positions 2 o and 2 o + 1 name blocks of two different groups of 4 consecutive blocks, and every such group is named at exactly two positions, of two different o.
All inputs are finite; a program needn't handle non-finite values.
Results may differ from the reference program's by a relative error of at most 0.0001.
Values sent between devices are 32-bit elements; how exact they have to be, the bound alone decides.
No kernel may reach another device: no remote copies, remote signals or barrier semaphores. Data moves between devices by JAX's collectives and lax.ppermute only.
A program may use at most 128 MiB of HBM per device.

```python
import math
import jax
import jax.numpy as jnp
import numpy as np
from jax import lax

ORDER = 16384
BS = 256
PC = 256
NSUP = 4
FRONTS = 2
KB = 32
MF = 8192
N_ROW = 8
N_COL = 16


def draw_front_blocks(key, part):
    block_count = ORDER // BS
    group_size = block_count // N_COL
    chosen_rows = []
    for front_index in range(2):
        front_key = jax.random.fold_in(key, 101 + front_index)
        subkeys = jax.random.split(front_key, 4)
        order_rows = jax.random.permutation(subkeys[0], N_ROW)
        offset = jax.random.randint(subkeys[1], (), 0, N_ROW)
        flip_bits = jax.random.randint(subkeys[2], (N_ROW,), 0, 2)
        within = jax.vmap(lambda subkey: jax.random.permutation(subkey, group_size))(jax.random.split(subkeys[3], N_COL))
        position = jnp.arange(KB)
        holder = position // 2
        second = position % 2
        row_holder = holder // 2
        shift_step = 2 * (holder % 2) + second
        region = order_rows[(row_holder + offset + shift_step) % N_ROW]
        column_group = 2 * region + (second + flip_bits[region]) % 2
        chosen = column_group * group_size + within[column_group, holder % 2]
        chosen_rows.append(chosen)
    return jnp.stack(chosen_rows).astype(jnp.int32)


def steps_of(key, shape, cuts, low, largest):
    def one(axis_at, blocks):
        heights = jax.random.uniform(jax.random.fold_in(jax.random.fold_in(key, 6), axis_at), (blocks,), jnp.float32, low / len(cuts), largest / len(cuts))
        return jnp.repeat(jnp.exp(heights), shape[axis_at] // blocks).reshape((-1,) + (1,) * (len(shape) - axis_at - 1))

    gain = one(*cuts[0])
    for cut in cuts[1:]:
        gain = gain * one(*cut)
    return gain


def profile(count, total, reach, slope):
    loads = [(1 << 20) // math.isqrt(standing ** slope) + 1 for standing in range(2, count + 1)]
    spare, holding = total - reach - (count - 1), [1] * (count - 1)
    while spare > 0:
        movable = [i for i in range(count - 1) if holding[i] < reach]
        mass, left = sum([loads[i] for i in movable]), spare
        for i in movable:
            extra = min(reach - holding[i], max(1, left * loads[i] // mass), spare)
            holding[i] = holding[i] + extra
            spare = spare - extra
    return np.array([reach] + holding)


def uneven(key, amount, total, most, skew):
    if amount == 2:
        one = jax.random.randint(key, (), max(1, total - most), min(most, total - 1) + 1)
        return jnp.stack([one, total - one])
    sizes = jnp.asarray(profile(amount, total, most, skew), jnp.int32)
    twos = (amount - 1) // 2
    donor, taker = sizes[1:1 + 2 * twos:2], sizes[2:2 + 2 * twos:2]
    margin = jnp.minimum(donor - 1, most - taker)
    passed = jax.random.randint(jax.random.fold_in(key, 1), (twos,), 0, 1 << 20) % (margin + 1)
    sizes = sizes.at[1:1 + 2 * twos:2].set(donor - passed).at[2:2 + 2 * twos:2].set(taker + passed)
    return sizes[jax.random.permutation(jax.random.fold_in(key, 2), amount)]


def centred(rng, extent, spread, bound, shards=(), held_as=jnp.bfloat16):
    values = jax.random.normal(rng, extent, jnp.float32) * spread
    if len(shards) > 0:
        values = steps_of(rng, extent, shards, -0.22, 0.18) * values
    return jnp.clip(values, min=-bound, max=bound).astype(held_as)


def setup_inputs(seed: int = 0) -> dict:
    key_of = jax.random.split(jax.random.key(seed), 6)
    return {
        "inverse": centred(key_of[0], (ORDER, ORDER), 1.0, 6.0, ((0, 8), (1, 16)), jnp.float32),
        "front_blocks": draw_front_blocks(jax.random.fold_in(key_of[5], 71), 0),
        "panels": centred(key_of[2], (FRONTS, MF, PC), MF ** -0.5, 0.0625, ((1, 8),), jnp.float32),
        "diag_terms": centred(key_of[3], (FRONTS, PC, PC), 1.0, 6.0, (), jnp.float32),
        "bounds": jax.vmap(lambda own: uneven(own, NSUP, PC, PC // 2, 2))(jax.random.split(key_of[4], FRONTS)).reshape((FRONTS, NSUP)).astype(jnp.int32),
    }


def reference(inverse, front_blocks, panels, diag_terms, bounds):
    block_count = ORDER // BS
    tile_grid = inverse.reshape(block_count, BS, block_count, BS)
    borders = []
    diagonals = []
    for front_index in range(2):
        front_list = front_blocks[front_index].astype(jnp.int32)
        front_inverse = jnp.take(tile_grid, front_list, axis=0)
        front_inverse = jnp.take(front_inverse, front_list, axis=2).reshape(MF, MF)
        border = -jnp.dot(front_inverse, panels[front_index], precision=lax.Precision.HIGHEST)
        node_ends = jnp.cumsum(bounds[front_index])
        columns = jnp.arange(PC, dtype=jnp.int32)
        node_ids = jnp.sum((columns[:, None] >= node_ends[None, :]).astype(jnp.int32), axis=1)
        same_node = (node_ids[:, None] == node_ids[None, :]).astype(jnp.float32)
        inner = jnp.dot(panels[front_index].T, border, precision=lax.Precision.HIGHEST)
        borders.append(border)
        diagonals.append(same_node * (diag_terms[front_index] - inner))
    return (jnp.stack(borders), jnp.stack(diagonals))
```

```python
import jax
import jax.numpy as jnp
from jax import lax
from jax.experimental import pallas as pl
from jax.experimental.pallas import tpu as pltpu
from jax.sharding import Mesh, PartitionSpec as P

F32 = jnp.float32
BF16 = jnp.bfloat16
ROW = ("y", "core")
COL = ("z", "x")
ALL = ("y", "core", "z", "x")
VMEM = pl.BlockSpec(memory_space=pltpu.VMEM)
SMEM = pl.BlockSpec(memory_space=pltpu.SMEM)
ANY = pl.BlockSpec(memory_space=pl.ANY)
PARAMS = pltpu.CompilerParams(vmem_limit_bytes=40 * 1024 * 1024)


def sds(shape, dtype=F32):
    return jax.ShapeDtypeStruct(shape, dtype)


def split(v):
    hi = v.astype(BF16)
    lo = (v - hi.astype(F32)).astype(BF16)
    return hi, lo


def dot3(a, b, dims):
    (ah, al), (bh, bl) = a, b
    mm = lambda p, q: lax.dot_general(p, q, (dims, ((), ())), preferred_element_type=F32)
    return mm(ah, bh) + (mm(ah, bl) + mm(al, bh))


def pack_kernel(fb, w, out, tab):
    r = lax.axis_index("y") * 2 + lax.axis_index("core")
    z, x = lax.axis_index("z"), lax.axis_index("x")
    c = z * 4 + x
    share = x * 64 + z * 16
    for f in range(2):
        own = [fb[f, 4 * r + i] for i in range(4)]
        piece = jnp.int32(0)
        for i in range(1, 4):
            piece = jnp.where((own[i] >> 2) == c, i, piece)
        for d in range(8):
            at = pl.multiple_of(piece * 256 + d * 32, 32)
            out[d, 32 * f : 32 * f + 32] = w[f, pl.ds(at, 32), :]
            named = jnp.int32(0)
            for i in range(1, 4):
                named = jnp.where((own[i] >> 3) == d, i, named)
            at = pl.multiple_of(named * 256 + share, 16)
            out[d, 64 + 16 * f : 80 + 16 * f] = w[f, pl.ds(at, 16), :]
    for k in range(32):
        tab[k] = 0
    for f in range(2):
        rows = jnp.int32(0)
        cols = jnp.int32(0)
        for p in range(32):
            b = fb[f, p]
            tab[16 * f + rows] = p
            rows = rows + ((b >> 3) == r).astype(jnp.int32)
            tab[16 * f + 8 + cols] = p
            cols = cols + ((b >> 2) == c).astype(jnp.int32)


def pick_kernel(tab, inc, slices, mine):
    for f in range(2):
        for t in range(2):
            p = tab[16 * f + 8 + t]
            slices[2 * f + t] = inc[p >> 2, 32 * f : 32 * f + 32, :]
        for s in range(4):
            p = tab[16 * f + s]
            mine[4 * f + s] = inc[p >> 2, 64 + 16 * f : 80 + 16 * f, :]


def product_kernel(fb, tab, inverse, w, out, tiles, sems):
    copies = []
    for f in range(2):
        for s in range(4):
            for t in range(2):
                k = (4 * f + s) * 2 + t
                rb = fb[f, tab[16 * f + s]] & 7
                cb = fb[f, tab[16 * f + 8 + t]] & 3
                src = inverse.at[
                    pl.ds(pl.multiple_of(rb * 256, 256), 256),
                    pl.ds(pl.multiple_of(cb * 256, 256), 256),
                ]
                copy = pltpu.make_async_copy(src, tiles.at[k], sems.at[k])
                copy.start()
                copies.append(copy)
    for f in range(2):
        ws = [split(w[:, 2 * f + t].reshape(256, 256)) for t in range(2)]
        for s in range(4):
            total = None
            for t in range(2):
                k = (4 * f + s) * 2 + t
                copies[k].wait()
                part = dot3(split(tiles[k]), ws[t], ((1,), (0,)))
                total = part if total is None else total + part
            for d in range(16):
                at = 64 * (d % 4) + 16 * (d // 4)
                out[d, 4 * f + s] = total[at : at + 16, :]


def same_node(bounds, f):
    a = lax.broadcasted_iota(jnp.int32, (256, 256), 0)
    b = lax.broadcasted_iota(jnp.int32, (256, 256), 1)
    ia = jnp.zeros((256, 256), jnp.int32)
    ib = jnp.zeros((256, 256), jnp.int32)
    end = jnp.int32(0)
    for k in range(4):
        end = end + bounds[f, k]
        ia = ia + (a >= end).astype(jnp.int32)
        ib = ib + (b >= end).astype(jnp.int32)
    return ia == ib


def reduce_kernel(tab, bounds, parts, mine, route, share):
    route[...] = jnp.zeros(route.shape, F32)
    for f in range(2):
        rows = []
        for s in range(4):
            v = parts[0, 4 * f + s]
            for d in range(1, 16):
                v = v + parts[d, 4 * f + s]
            rows.append(v)
            route[tab[16 * f + s] >> 2, f] = -v
        left = mine[4 * f : 4 * f + 4].reshape(64, 256)
        right = jnp.concatenate(rows, axis=0)
        full = dot3(split(left), split(right), ((0,), (0,)))
        full = jnp.where(same_node(bounds, f), full, 0.0)
        packed = full[:, :128] + full[:, 128:]
        share[64 * f : 64 * f + 64] = packed.reshape(64, 4, 128)


def place_kernel(fb, inc, out):
    r = lax.axis_index("y") * 2 + lax.axis_index("core")
    for f in range(2):
        for i in range(4):
            out[i, f] = inc[fb[f, 4 * r + i] >> 3, f]


def spread_kernel(inc, out):
    total = jnp.sum(inc[...], axis=0)
    out[...] = jnp.broadcast_to(total[None], out.shape)


def finish_kernel(bounds, packed, terms, out):
    for f in range(2):
        v = packed[64 * f : 64 * f + 64].reshape(256, 128)
        full = terms[f] + jnp.concatenate([v, v], axis=1)
        out[f] = jnp.where(same_node(bounds, f), full, 0.0)


def call(kernel, ins, out_shape, out_specs=None, scratch=()):
    if out_specs is None:
        out_specs = jax.tree.map(lambda _: VMEM, out_shape)
    return pl.pallas_call(
        kernel,
        in_specs=ins,
        out_shape=out_shape,
        out_specs=out_specs,
        scratch_shapes=scratch,
        compiler_params=PARAMS,
    )


def body(inverse, fb, panels, terms, bounds):
    a2a = lambda v, axes: lax.all_to_all(v, axes, 0, 0, tiled=True)
    outgoing, tab = call(
        pack_kernel, [SMEM, VMEM], (sds((8, 96, 256)), sds((32,), jnp.int32)), (VMEM, SMEM)
    )(fb, panels)
    incoming = a2a(outgoing, ROW)
    slices, mine = call(
        pick_kernel, [SMEM, VMEM], (sds((4, 32, 256)), sds((8, 16, 256)))
    )(tab, incoming)
    w = lax.all_gather(slices, ROW, axis=0, tiled=False)
    parts = call(
        product_kernel,
        [SMEM, SMEM, ANY, VMEM],
        sds((16, 8, 16, 256)),
        scratch=[pltpu.VMEM((16, 256, 256), F32), pltpu.SemaphoreType.DMA((16,))],
    )(fb, tab, inverse, w.reshape(8, 4, 32, 256))
    parts = a2a(parts, COL)
    route, share = call(
        reduce_kernel,
        [SMEM, SMEM, VMEM, VMEM],
        (sds((8, 2, 16, 256)), sds((128, 4, 128))),
    )(tab, bounds, parts, mine)
    share = a2a(share, ALL)
    route = a2a(route, ROW)
    route = call(place_kernel, [SMEM, VMEM], sds((4, 2, 16, 256)))(fb, route)
    border = a2a(route, "z").transpose(1, 0, 2, 3).reshape(2, 64, 256)
    share = call(spread_kernel, [VMEM], sds((128, 4, 128)))(share)
    packed = a2a(share, ALL)
    diag = call(finish_kernel, [SMEM, VMEM, VMEM], sds((2, 256, 256)))(bounds, packed, terms)
    return border, diag


def solution(mesh):
    grid = Mesh(mesh.devices.reshape(4, 2, 4, 4), ALL)
    placed = (P(ROW, COL), P(), P(None, ROW, None), P(), P())
    return jax.shard_map(
        body,
        mesh=grid,
        in_specs=placed,
        out_specs=(P(None, ALL, None), P()),
        check_vma=False,
    )
```

```python
import jax
import jax.numpy as jnp
from jax import lax
from jax.experimental import pallas as pl
from jax.experimental.pallas import tpu as pltpu
from jax.sharding import Mesh, PartitionSpec as P

F32 = jnp.float32
BF16 = jnp.bfloat16
ROW = ("y", "core")
COL = ("z", "x")
ALL = ("y", "core", "z", "x")
VMEM = pl.BlockSpec(memory_space=pltpu.VMEM)
SMEM = pl.BlockSpec(memory_space=pltpu.SMEM)
ANY = pl.BlockSpec(memory_space=pl.ANY)
HBM = pl.BlockSpec(memory_space=pltpu.HBM)
MIB = 1024 * 1024


def sds(shape, dtype=F32):
    return jax.ShapeDtypeStruct(shape, dtype)


def split(v):
    hi = v.astype(BF16)
    lo = (v - hi.astype(F32)).astype(BF16)
    return hi, lo


def dot3(a, b, dims):
    (ah, al), (bh, bl) = a, b
    mm = lambda p, q: lax.dot_general(p, q, (dims, ((), ())), preferred_element_type=F32)
    return mm(ah, bh) + (mm(ah, bl) + mm(al, bh))


def pack_kernel(fb, w, out, tab):
    r = lax.axis_index("y") * 2 + lax.axis_index("core")
    z, x = lax.axis_index("z"), lax.axis_index("x")
    c = z * 4 + x
    share = x * 64 + z * 16
    for f in range(2):
        own = [fb[f, 4 * r + i] for i in range(4)]
        piece = jnp.int32(0)
        for i in range(1, 4):
            piece = jnp.where((own[i] >> 2) == c, i, piece)
        for d in range(8):
            at = pl.multiple_of(piece * 256 + (d % 2 * 4 + d // 2) * 32, 32)
            out[d, 32 * f : 32 * f + 32] = w[f, pl.ds(at, 32), :]
            named = jnp.int32(0)
            for i in range(1, 4):
                named = jnp.where((own[i] >> 3) == d, i, named)
            at = pl.multiple_of(named * 256 + share, 16)
            out[d, 64 + 16 * f : 80 + 16 * f] = w[f, pl.ds(at, 16), :]
    for k in range(32):
        tab[k] = 0
    for f in range(2):
        rows = jnp.int32(0)
        cols = jnp.int32(0)
        for p in range(32):
            b = fb[f, p]
            tab[16 * f + rows] = p
            rows = rows + ((b >> 3) == r).astype(jnp.int32)
            tab[16 * f + 8 + cols] = p
            cols = cols + ((b >> 2) == c).astype(jnp.int32)


def pick_kernel(tab, inc, after, slices, mine):
    for f in range(2):
        for t in range(2):
            p = tab[16 * f + 8 + t]
            v = inc[p >> 2, 32 * f : 32 * f + 32, :]
            for d in range(4):
                slices[d, 2 * f + t] = v
        for s in range(4):
            p = tab[16 * f + s]
            mine[4 * f + s] = inc[p >> 2, 64 + 16 * f : 80 + 16 * f, :]


def tile_kernel(fb, tab, inverse, hi, lo, tiles, sems):
    copies = []
    for f in range(2):
        for s in range(4):
            for t in range(2):
                k = (4 * f + s) * 2 + t
                rb = fb[f, tab[16 * f + s]] & 7
                cb = fb[f, tab[16 * f + 8 + t]] & 3
                src = inverse.at[
                    pl.ds(pl.multiple_of(rb * 256, 256), 256),
                    pl.ds(pl.multiple_of(cb * 256, 256), 256),
                ]
                copy = pltpu.make_async_copy(src, tiles.at[k], sems.at[k])
                copy.start()
                copies.append(copy)
    for k in range(16):
        copies[k].wait()
        h, l = split(tiles[k])
        hi[k // 2, :, 256 * (k % 2) : 256 * (k % 2) + 256] = h
        lo[k // 2, :, 256 * (k % 2) : 256 * (k % 2) + 256] = l


def product_kernel(hi, lo, own, other, out, whole):
    core = lax.axis_index("core")
    for k in range(4):
        base = 256 * (k % 2)
        at = pl.multiple_of(base + 128 * core, 128)
        whole[k // 2, pl.ds(at, 128), :] = own[:, k].reshape(128, 256)
        at = pl.multiple_of(base + 128 * (1 - core), 128)
        whole[k // 2, pl.ds(at, 128), :] = other[:, k].reshape(128, 256)
    for f in range(2):
        w = split(whole[f])
        for s in range(4):
            total = dot3((hi[4 * f + s], lo[4 * f + s]), w, ((1,), (0,)))
            for d in range(16):
                at = 64 * (d % 4) + 16 * (d // 4)
                out[d, 4 * f + s] = total[at : at + 16, :]


def same_node(bounds, f):
    a = lax.broadcasted_iota(jnp.int32, (256, 256), 0)
    b = lax.broadcasted_iota(jnp.int32, (256, 256), 1)
    ia = jnp.zeros((256, 256), jnp.int32)
    ib = jnp.zeros((256, 256), jnp.int32)
    end = jnp.int32(0)
    for k in range(4):
        end = end + bounds[f, k]
        ia = ia + (a >= end).astype(jnp.int32)
        ib = ib + (b >= end).astype(jnp.int32)
    return ia == ib


def reduce_kernel(tab, bounds, parts, mine, out):
    for d in range(8):
        out[d, 0:32] = jnp.zeros((32, 256), F32)
    for f in range(2):
        rows = []
        for s in range(4):
            v = parts[0, 4 * f + s]
            for d in range(1, 16):
                v = v + parts[d, 4 * f + s]
            rows.append(v)
            out[tab[16 * f + s] >> 2, 16 * f : 16 * f + 16] = -v
        left = mine[4 * f : 4 * f + 4].reshape(64, 256)
        right = jnp.concatenate(rows, axis=0)
        full = dot3(split(left), split(right), ((0,), (0,)))
        full = jnp.where(same_node(bounds, f), full, 0.0)
        packed = full[:, :128] + full[:, 128:]
        for d in range(4):
            part = packed[64 * d : 64 * d + 64]
            out[4 * f + d, 32:64] = jnp.concatenate([part[:32], part[32:]], axis=1)


def place_kernel(fb, inc, out):
    r = lax.axis_index("y") * 2 + lax.axis_index("core")
    x = lax.axis_index("x")
    total = inc[0, 32:64]
    for d in range(1, 8):
        total = total + inc[d, 32:64]
    for d in range(16):
        out[d, 0:32] = jnp.zeros((32, 256), F32)
        out[d, 32:64] = total
    for f in range(2):
        for i in range(4):
            v = inc[fb[f, 4 * r + i] >> 3, 16 * f : 16 * f + 16, :]
            out[4 * i + x, 16 * f : 16 * f + 16] = v


def border_kernel(inc, border, out):
    x = lax.axis_index("x")
    for z in range(4):
        for f in range(2):
            border[f, 16 * z : 16 * z + 16] = inc[4 * z + x, 16 * f : 16 * f + 16, :]
    total = inc[0, 32:64]
    for d in range(1, 16):
        total = total + inc[d, 32:64]
    for d in range(4):
        out[d] = total


def finish_kernel(bounds, own, other, terms, out, chunks):
    core = lax.axis_index("core")
    for y in range(4):
        chunks[2 * y + core] = own[y]
        chunks[2 * y + 1 - core] = other[y]
    for f in range(2):
        same = same_node(bounds, f)
        for d in range(4):
            v = chunks[4 * f + d]
            v = jnp.concatenate([v[:, :128], v[:, 128:]], axis=0)
            at = slice(64 * d, 64 * d + 64)
            full = terms[f, at] + jnp.concatenate([v, v], axis=1)
            out[f, at] = jnp.where(same[at], full, 0.0)


def call(kernel, ins, out_shape, out_specs=None, scratch=(), limit=40, cost=None):
    if out_specs is None:
        out_specs = jax.tree.map(lambda _: VMEM, out_shape)
    return pl.pallas_call(
        kernel,
        in_specs=ins,
        out_shape=out_shape,
        out_specs=out_specs,
        scratch_shapes=scratch,
        cost_estimate=cost,
        compiler_params=pltpu.CompilerParams(vmem_limit_bytes=limit * MIB),
    )


def a2a(v, axes):
    return lax.all_to_all(v, axes, 0, 0, tiled=True)


def swap(v):
    return lax.ppermute(v, "core", [(0, 1), (1, 0)])


def body(inverse, fb, panels, terms, bounds):
    outgoing, tab = call(
        pack_kernel, [SMEM, VMEM], (sds((8, 96, 256)), sds((32,), jnp.int32)), (VMEM, SMEM)
    )(fb, panels)
    incoming = a2a(outgoing, ROW)
    hi, lo = call(
        tile_kernel,
        [SMEM, SMEM, HBM],
        (sds((8, 256, 512), BF16), sds((8, 256, 512), BF16)),
        scratch=[pltpu.VMEM((16, 256, 256), F32), pltpu.SemaphoreType.DMA((16,))],
        limit=52,
        cost=pl.CostEstimate(flops=4 * MIB, bytes_accessed=12 * MIB, transcendentals=0),
    )(fb, tab, inverse)
    slices, mine = call(
        pick_kernel, [SMEM, VMEM, ANY], (sds((4, 4, 32, 256)), sds((8, 16, 256)))
    )(tab, incoming, hi)
    own = a2a(slices, "y")
    other = swap(own)
    parts = call(
        product_kernel,
        [VMEM, VMEM, VMEM, VMEM],
        sds((16, 8, 16, 256)),
        scratch=[pltpu.VMEM((2, 512, 256), F32)],
    )(hi, lo, own, other)
    parts = a2a(parts, COL)
    v = call(reduce_kernel, [SMEM, SMEM, VMEM, VMEM], sds((8, 64, 256)))(tab, bounds, parts, mine)
    v = a2a(v, ROW)
    v = call(place_kernel, [SMEM, VMEM], sds((16, 64, 256)))(fb, v)
    v = a2a(v, COL)
    border, v = call(border_kernel, [VMEM], (sds((2, 64, 256)), sds((4, 32, 256))))(v)
    own = a2a(v, "y")
    other = swap(own)
    diag = call(
        finish_kernel,
        [SMEM, VMEM, VMEM, VMEM],
        sds((2, 256, 256)),
        scratch=[pltpu.VMEM((8, 32, 256), F32)],
    )(bounds, own, other, terms)
    return border, diag


def solution(mesh):
    grid = Mesh(mesh.devices.reshape(4, 2, 4, 4), ALL)
    placed = (P(ROW, COL), P(), P(None, ROW, None), P(), P())
    return jax.shard_map(
        body,
        mesh=grid,
        in_specs=placed,
        out_specs=(P(None, ALL, None), P()),
        check_vma=False,
    )
```

```python
import jax
import jax.numpy as jnp
from jax import lax
from jax.experimental import pallas as pl
from jax.experimental.pallas import tpu as pltpu
from jax.sharding import Mesh, PartitionSpec as P

F32 = jnp.float32
BF16 = jnp.bfloat16
ROW = ("y", "core")
COL = ("z", "x")
ALL = ("y", "core", "z", "x")
VMEM = pl.BlockSpec(memory_space=pltpu.VMEM)
SMEM = pl.BlockSpec(memory_space=pltpu.SMEM)
ANY = pl.BlockSpec(memory_space=pl.ANY)
MIB = 1024 * 1024


def sds(shape, dtype=F32):
    return jax.ShapeDtypeStruct(shape, dtype)


def split(v):
    hi = v.astype(BF16)
    lo = (v - hi.astype(F32)).astype(BF16)
    return hi, lo


def dot3(a, b, dims):
    (ah, al), (bh, bl) = a, b
    mm = lambda p, q: lax.dot_general(p, q, (dims, ((), ())), preferred_element_type=F32)
    return mm(ah, bh) + (mm(ah, bl) + mm(al, bh))


def pack_kernel(fb, w, out, tab, sems):
    r = lax.axis_index("y") * 2 + lax.axis_index("core")
    z, x = lax.axis_index("z"), lax.axis_index("x")
    c = z * 4 + x
    part = 2 * x + z // 2
    row = pl.multiple_of(16 * (z % 2), 16)
    copies = []

    def start(src, dst):
        copy = pltpu.make_async_copy(src, dst, sems.at[len(copies)])
        copy.start()
        copies.append(copy)

    for f in range(2):
        own = [fb[f, 4 * r + i] for i in range(4)]
        piece = jnp.int32(0)
        for i in range(1, 4):
            piece = jnp.where((own[i] >> 2) == c, i, piece)
        for k in range(2):
            start(w.at[f, piece, k], out.at[:, k, 32 * f : 32 * f + 32])
        for d in range(8):
            named = jnp.int32(0)
            for i in range(1, 4):
                named = jnp.where((own[i] >> 3) == d, i, named)
            start(
                w.at[f, named, part // 4, part % 4, pl.ds(row, 16)],
                out.at[d // 2, d % 2, 64 + 16 * f : 80 + 16 * f],
            )
    for k in range(32):
        tab[k] = 0
    for f in range(2):
        rows = jnp.int32(0)
        cols = jnp.int32(0)
        for p in range(32):
            b = fb[f, p]
            tab[16 * f + rows] = p
            rows = rows + ((b >> 3) == r).astype(jnp.int32)
            tab[16 * f + 8 + cols] = p
            cols = cols + ((b >> 2) == c).astype(jnp.int32)
    for copy in copies:
        copy.wait()


def pick_kernel(tab, inc, after, slices, mine):
    for f in range(2):
        for t in range(2):
            p = tab[16 * f + 8 + t]
            v = inc[p >> 2, 32 * f : 32 * f + 32, :]
            for d in range(4):
                slices[d, 2 * f + t] = v
        for s in range(4):
            p = tab[16 * f + s]
            mine[4 * f + s] = inc[p >> 2, 64 + 16 * f : 80 + 16 * f, :]


def tile_kernel(fb, tab, inverse, hi, lo, tiles, sems):
    copies = []
    for f in range(2):
        for s in range(4):
            for t in range(2):
                k = (4 * f + s) * 2 + t
                rb = fb[f, tab[16 * f + s]] & 7
                cb = fb[f, tab[16 * f + 8 + t]] & 3
                src = inverse.at[
                    pl.ds(pl.multiple_of(rb * 256, 256), 256),
                    pl.ds(pl.multiple_of(cb * 256, 256), 256),
                ]
                copy = pltpu.make_async_copy(src, tiles.at[k], sems.at[k])
                copy.start()
                copies.append(copy)
    for k in range(16):
        copies[k].wait()
        h, l = split(tiles[k])
        hi[k // 2, :, 256 * (k % 2) : 256 * (k % 2) + 256] = h
        lo[k // 2, :, 256 * (k % 2) : 256 * (k % 2) + 256] = l


def product_kernel(hi, lo, own, other, out, whole):
    core = lax.axis_index("core")
    for k in range(4):
        base = 256 * (k % 2)
        at = pl.multiple_of(base + 128 * core, 128)
        whole[k // 2, pl.ds(at, 128), :] = own[:, k].reshape(128, 256)
        at = pl.multiple_of(base + 128 * (1 - core), 128)
        whole[k // 2, pl.ds(at, 128), :] = other[:, k].reshape(128, 256)
    for f in range(2):
        w = split(whole[f])
        for s in range(4):
            total = dot3((hi[4 * f + s], lo[4 * f + s]), w, ((1,), (0,)))
            for d in range(16):
                at = 64 * (d % 4) + 16 * (d // 4)
                out[d, 4 * f + s] = total[at : at + 16, :]


def same_node(bounds, f):
    a = lax.broadcasted_iota(jnp.int32, (256, 256), 0)
    b = lax.broadcasted_iota(jnp.int32, (256, 256), 1)
    ia = jnp.zeros((256, 256), jnp.int32)
    ib = jnp.zeros((256, 256), jnp.int32)
    end = jnp.int32(0)
    for k in range(4):
        end = end + bounds[f, k]
        ia = ia + (a >= end).astype(jnp.int32)
        ib = ib + (b >= end).astype(jnp.int32)
    return ia == ib


def reduce_kernel(tab, bounds, parts, mine, out):
    for d in range(8):
        out[d, 0:32] = jnp.zeros((32, 256), F32)
    for f in range(2):
        rows = []
        for s in range(4):
            v = parts[0, 4 * f + s]
            for d in range(1, 16):
                v = v + parts[d, 4 * f + s]
            rows.append(v)
            out[tab[16 * f + s] >> 2, 16 * f : 16 * f + 16] = -v
        left = mine[4 * f : 4 * f + 4].reshape(64, 256)
        right = jnp.concatenate(rows, axis=0)
        full = dot3(split(left), split(right), ((0,), (0,)))
        full = jnp.where(same_node(bounds, f), full, 0.0)
        packed = full[:, :128] + full[:, 128:]
        for d in range(4):
            part = packed[64 * d : 64 * d + 64]
            out[4 * f + d, 32:64] = jnp.concatenate([part[:32], part[32:]], axis=1)


def place_kernel(fb, inc, route, share):
    r = lax.axis_index("y") * 2 + lax.axis_index("core")
    total = inc[0, 32:64]
    for d in range(1, 8):
        total = total + inc[d, 32:64]
    for d in range(4):
        share[d] = total
    for f in range(2):
        for i in range(4):
            route[i, 16 * f : 16 * f + 16] = inc[fb[f, 4 * r + i] >> 3, 16 * f : 16 * f + 16, :]


def join_kernel(route, share, out):
    total = (share[0] + share[1]) + (share[2] + share[3])
    for d in range(4):
        out[d, 0:32] = route[d]
        out[d, 32:64] = total


def border_kernel(inc, border, out):
    for z in range(4):
        for f in range(2):
            border[f, 16 * z : 16 * z + 16] = inc[z, 16 * f : 16 * f + 16, :]
    total = (inc[0, 32:64] + inc[1, 32:64]) + (inc[2, 32:64] + inc[3, 32:64])
    for d in range(4):
        out[d] = total


def finish_kernel(bounds, own, other, terms, out, chunks):
    core = lax.axis_index("core")
    for y in range(4):
        chunks[2 * y + core] = own[y]
        chunks[2 * y + 1 - core] = other[y]
    for f in range(2):
        same = same_node(bounds, f)
        for d in range(4):
            v = chunks[4 * f + d]
            v = jnp.concatenate([v[:, :128], v[:, 128:]], axis=0)
            at = slice(64 * d, 64 * d + 64)
            full = terms[f, at] + jnp.concatenate([v, v], axis=1)
            out[f, at] = jnp.where(same[at], full, 0.0)


def call(kernel, ins, out_shape, out_specs=None, scratch=(), limit=40, cost=None):
    if out_specs is None:
        out_specs = jax.tree.map(lambda _: VMEM, out_shape)
    return pl.pallas_call(
        kernel,
        in_specs=ins,
        out_shape=out_shape,
        out_specs=out_specs,
        scratch_shapes=scratch,
        cost_estimate=cost,
        compiler_params=pltpu.CompilerParams(vmem_limit_bytes=limit * MIB),
    )


def a2a(v, axes):
    return lax.all_to_all(v, axes, 0, 0, tiled=True)


def hbm(v):
    return pltpu.with_memory_space_constraint(v, pltpu.HBM)


def swap(v):
    return lax.ppermute(v, "core", [(0, 1), (1, 0)])


def body(inverse, fb, panels, terms, bounds):
    outgoing, tab = call(
        pack_kernel,
        [SMEM, ANY],
        (sds((4, 2, 96, 256)), sds((32,), jnp.int32)),
        (VMEM, SMEM),
        scratch=[pltpu.SemaphoreType.DMA((20,))],
    )(hbm(fb), hbm(panels.reshape(2, 4, 2, 4, 32, 256)))
    incoming = a2a(outgoing.reshape(8, 96, 256), ROW)
    hi, lo = call(
        tile_kernel,
        [SMEM, SMEM, ANY],
        (sds((8, 256, 512), BF16), sds((8, 256, 512), BF16)),
        scratch=[pltpu.VMEM((16, 256, 256), F32), pltpu.SemaphoreType.DMA((16,))],
        limit=24,
        cost=pl.CostEstimate(flops=4 * MIB, bytes_accessed=12 * MIB, transcendentals=0),
    )(fb, tab, hbm(inverse))
    slices, mine = call(
        pick_kernel, [SMEM, VMEM, ANY], (sds((4, 4, 32, 256)), sds((8, 16, 256)))
    )(tab, incoming, hi)
    own = a2a(slices, "y")
    other = swap(own)
    parts = call(
        product_kernel,
        [VMEM, VMEM, VMEM, VMEM],
        sds((16, 8, 16, 256)),
        scratch=[pltpu.VMEM((2, 512, 256), F32)],
    )(hi, lo, own, other)
    parts = a2a(parts, COL)
    v = call(reduce_kernel, [SMEM, SMEM, VMEM, VMEM], sds((8, 64, 256)))(tab, bounds, parts, mine)
    v = a2a(v, ROW)
    route, v = call(place_kernel, [SMEM, VMEM], (sds((4, 32, 256)), sds((4, 32, 256))))(fb, v)
    v = a2a(v, "x")
    v = call(join_kernel, [VMEM, VMEM], sds((4, 64, 256)))(route, v)
    v = a2a(v, "z")
    border, v = call(border_kernel, [VMEM], (sds((2, 64, 256)), sds((4, 32, 256))))(v)
    own = a2a(v, "y")
    other = swap(own)
    diag = call(
        finish_kernel,
        [SMEM, VMEM, VMEM, VMEM],
        sds((2, 256, 256)),
        scratch=[pltpu.VMEM((8, 32, 256), F32)],
    )(bounds, own, other, terms)
    return border, diag


def solution(mesh):
    grid = Mesh(mesh.devices.reshape(4, 2, 4, 4), ALL)
    placed = (P(ROW, COL), P(), P(None, ROW, None), P(), P())
    return jax.shard_map(
        body,
        mesh=grid,
        in_specs=placed,
        out_specs=(P(None, ALL, None), P()),
        check_vma=False,
    )
```

```python
import jax
import jax.numpy as jnp
from jax import lax
from jax.experimental import pallas as pl
from jax.experimental.pallas import tpu as pltpu
from jax.sharding import Mesh, PartitionSpec as P

F32 = jnp.float32
BF16 = jnp.bfloat16
ROW = ("y", "core")
COL = ("z", "x")
ALL = ("y", "core", "z", "x")
VMEM = pl.BlockSpec(memory_space=pltpu.VMEM)
SMEM = pl.BlockSpec(memory_space=pltpu.SMEM)
ANY = pl.BlockSpec(memory_space=pl.ANY)
MIB = 1024 * 1024


def sds(shape, dtype=F32):
    return jax.ShapeDtypeStruct(shape, dtype)


def split(v):
    hi = v.astype(BF16)
    lo = (v - hi.astype(F32)).astype(BF16)
    return hi, lo


def dot3(a, b, dims):
    (ah, al), (bh, bl) = a, b
    mm = lambda p, q: lax.dot_general(p, q, (dims, ((), ())), preferred_element_type=F32)
    return mm(ah, bh) + (mm(ah, bl) + mm(al, bh))


def pack_kernel(fb, w, out, sems):
    r = lax.axis_index("y") * 2 + lax.axis_index("core")
    z, x = lax.axis_index("z"), lax.axis_index("x")
    c = z * 4 + x
    part = 2 * x + z // 2
    row = pl.multiple_of(16 * (z % 2), 16)
    copies = []

    def start(src, dst):
        copy = pltpu.make_async_copy(src, dst, sems.at[len(copies)])
        copy.start()
        copies.append(copy)

    for f in range(2):
        own = [fb[f, 4 * r + i] for i in range(4)]
        piece = jnp.int32(0)
        for i in range(1, 4):
            piece = jnp.where((own[i] >> 2) == c, i, piece)
        for k in range(2):
            start(w.at[f, piece, k], out.at[:, k, 32 * f : 32 * f + 32])
        for d in range(8):
            named = jnp.int32(0)
            for i in range(1, 4):
                named = jnp.where((own[i] >> 3) == d, i, named)
            start(
                w.at[f, named, part // 4, part % 4, pl.ds(row, 16)],
                out.at[d // 2, d % 2, 64 + 16 * f : 80 + 16 * f],
            )
    for copy in copies:
        copy.wait()


def pick_kernel(tab, inc, slices, mine):
    for f in range(2):
        for t in range(2):
            p = tab[16 * f + 8 + t]
            v = inc[p >> 2, 32 * f : 32 * f + 32, :]
            for d in range(4):
                slices[d, 2 * f + t] = v
        for s in range(4):
            p = tab[16 * f + s]
            mine[4 * f + s] = inc[p >> 2, 64 + 16 * f : 80 + 16 * f, :]


def same_node(bounds, f):
    a = lax.broadcasted_iota(jnp.int32, (256, 256), 0)
    b = lax.broadcasted_iota(jnp.int32, (256, 256), 1)
    ia = jnp.zeros((256, 256), jnp.int32)
    ib = jnp.zeros((256, 256), jnp.int32)
    end = jnp.int32(0)
    for k in range(4):
        end = end + bounds[f, k]
        ia = ia + (a >= end).astype(jnp.int32)
        ib = ib + (b >= end).astype(jnp.int32)
    return ia == ib


def tile_kernel(fb, bounds, terms, inverse, hi, lo, tab, mask, base, tiles, sems):
    r = lax.axis_index("y") * 2 + lax.axis_index("core")
    c = lax.axis_index("z") * 4 + lax.axis_index("x")
    for k in range(32):
        tab[k] = 0
    copies = []
    for f in range(2):
        rows = jnp.int32(0)
        cols = jnp.int32(0)
        for p in range(32):
            b = fb[f, p]
            tab[16 * f + rows] = p
            rows = rows + ((b >> 3) == r).astype(jnp.int32)
            tab[16 * f + 8 + cols] = p
            cols = cols + ((b >> 2) == c).astype(jnp.int32)
        for s in range(4):
            for t in range(2):
                k = (4 * f + s) * 2 + t
                rb = fb[f, tab[16 * f + s]] & 7
                cb = fb[f, tab[16 * f + 8 + t]] & 3
                src = inverse.at[
                    pl.ds(pl.multiple_of(rb * 256, 256), 256),
                    pl.ds(pl.multiple_of(cb * 256, 256), 256),
                ]
                copy = pltpu.make_async_copy(src, tiles.at[k], sems.at[k])
                copy.start()
                copies.append(copy)
    for f in range(2):
        same = same_node(bounds, f)
        mask[f] = same.astype(F32)
        base[f] = jnp.where(same, terms[f], 0.0)
    for k in range(16):
        copies[k].wait()
        h, l = split(tiles[k])
        hi[k // 2, :, 256 * (k % 2) : 256 * (k % 2) + 256] = h
        lo[k // 2, :, 256 * (k % 2) : 256 * (k % 2) + 256] = l


def product_kernel(hi, lo, own, other, out, whole):
    core = lax.axis_index("core")
    for k in range(4):
        base = 256 * (k % 2)
        at = pl.multiple_of(base + 128 * core, 128)
        whole[k // 2, pl.ds(at, 128), :] = own[:, k].reshape(128, 256)
        at = pl.multiple_of(base + 128 * (1 - core), 128)
        whole[k // 2, pl.ds(at, 128), :] = other[:, k].reshape(128, 256)
    for f in range(2):
        w = split(whole[f])
        for s in range(4):
            total = dot3((hi[4 * f + s], lo[4 * f + s]), w, ((1,), (0,)))
            for d in range(16):
                at = 64 * (d % 4) + 16 * (d // 4)
                out[d, 4 * f + s] = total[at : at + 16, :]


def reduce_kernel(tab, mask, parts, mine, out):
    for d in range(8):
        out[d, 0:32] = jnp.zeros((32, 256), F32)
    for f in range(2):
        rows = []
        for s in range(4):
            v = parts[0, 4 * f + s]
            for d in range(1, 16):
                v = v + parts[d, 4 * f + s]
            rows.append(v)
            out[tab[16 * f + s] >> 2, 16 * f : 16 * f + 16] = -v
        left = mine[4 * f : 4 * f + 4].reshape(64, 256)
        right = jnp.concatenate(rows, axis=0)
        full = dot3(split(left), split(right), ((0,), (0,)))
        full = full * mask[f]
        packed = full[:, :128] + full[:, 128:]
        for d in range(4):
            part = packed[64 * d : 64 * d + 64]
            out[4 * f + d, 32:64] = jnp.concatenate([part[:32], part[32:]], axis=1)


def place_kernel(fb, inc, out):
    r = lax.axis_index("y") * 2 + lax.axis_index("core")
    total = inc[0, 32:64]
    for d in range(1, 8):
        total = total + inc[d, 32:64]
    for d in range(4):
        out[d, 32:64] = total
    for f in range(2):
        for i in range(4):
            out[i, 16 * f : 16 * f + 16] = inc[fb[f, 4 * r + i] >> 3, 16 * f : 16 * f + 16, :]


def border_kernel(inc, border, out):
    for z in range(4):
        for f in range(2):
            border[f, 16 * z : 16 * z + 16] = inc[z, 16 * f : 16 * f + 16, :]
    total = (inc[0, 32:64] + inc[1, 32:64]) + (inc[2, 32:64] + inc[3, 32:64])
    for d in range(16):
        out[d] = total


def chunk_kernel(inc, out):
    for y in range(4):
        at = 4 * y
        out[y] = (inc[at] + inc[at + 1]) + (inc[at + 2] + inc[at + 3])


def finish_kernel(own, other, mask, base, out, chunks):
    core = lax.axis_index("core")
    for y in range(4):
        chunks[2 * y + core] = own[y]
        chunks[2 * y + 1 - core] = other[y]
    for f in range(2):
        for d in range(4):
            v = chunks[4 * f + d]
            v = jnp.concatenate([v[:, :128], v[:, 128:]], axis=0)
            at = slice(64 * d, 64 * d + 64)
            out[f, at] = base[f, at] + mask[f, at] * jnp.concatenate([v, v], axis=1)


def call(kernel, ins, out_shape, out_specs=None, scratch=(), limit=40, cost=None):
    if out_specs is None:
        out_specs = jax.tree.map(lambda _: VMEM, out_shape)
    return pl.pallas_call(
        kernel,
        in_specs=ins,
        out_shape=out_shape,
        out_specs=out_specs,
        scratch_shapes=scratch,
        cost_estimate=cost,
        compiler_params=pltpu.CompilerParams(vmem_limit_bytes=limit * MIB),
    )


def a2a(v, axes):
    return lax.all_to_all(v, axes, 0, 0, tiled=True)


def hbm(v):
    return pltpu.with_memory_space_constraint(v, pltpu.HBM)


def swap(v):
    return lax.ppermute(v, "core", [(0, 1), (1, 0)])


def body(inverse, fb, panels, terms, bounds):
    outgoing = call(
        pack_kernel,
        [SMEM, ANY],
        sds((4, 2, 96, 256)),
        scratch=[pltpu.SemaphoreType.DMA((20,))],
    )(hbm(fb), hbm(panels.reshape(2, 4, 2, 4, 32, 256)))
    incoming = a2a(outgoing.reshape(8, 96, 256), ROW)
    hi, lo, tab, mask, base = call(
        tile_kernel,
        [SMEM, SMEM, VMEM, ANY],
        (
            sds((8, 256, 512), BF16),
            sds((8, 256, 512), BF16),
            sds((32,), jnp.int32),
            sds((2, 256, 256)),
            sds((2, 256, 256)),
        ),
        (VMEM, VMEM, SMEM, VMEM, VMEM),
        scratch=[pltpu.VMEM((16, 256, 256), F32), pltpu.SemaphoreType.DMA((16,))],
        limit=24,
        cost=pl.CostEstimate(flops=4 * MIB, bytes_accessed=12 * MIB, transcendentals=0),
    )(fb, bounds, terms, hbm(inverse))
    slices, mine = call(
        pick_kernel, [SMEM, VMEM], (sds((4, 4, 32, 256)), sds((8, 16, 256)))
    )(tab, incoming)
    own = a2a(slices, "y")
    other = swap(own)
    parts = call(
        product_kernel,
        [VMEM, VMEM, VMEM, VMEM],
        sds((16, 8, 16, 256)),
        scratch=[pltpu.VMEM((2, 512, 256), F32)],
    )(hi, lo, own, other)
    parts = a2a(parts, COL)
    v = call(reduce_kernel, [SMEM, VMEM, VMEM, VMEM], sds((8, 64, 256)))(tab, mask, parts, mine)
    v = a2a(v, ROW)
    v = call(place_kernel, [SMEM, VMEM], sds((4, 64, 256)))(fb, v)
    v = a2a(v, "z")
    border, v = call(border_kernel, [VMEM], (sds((2, 64, 256)), sds((16, 32, 256))))(v)
    v = a2a(v, ("y", "x"))
    own = call(chunk_kernel, [VMEM], sds((4, 32, 256)))(v)
    other = swap(own)
    diag = call(
        finish_kernel,
        [VMEM, VMEM, VMEM, VMEM],
        sds((2, 256, 256)),
        scratch=[pltpu.VMEM((8, 32, 256), F32)],
    )(own, other, mask, base)
    return border, diag


def solution(mesh):
    grid = Mesh(mesh.devices.reshape(4, 2, 4, 4), ALL)
    placed = (P(ROW, COL), P(), P(None, ROW, None), P(), P())
    return jax.shard_map(
        body,
        mesh=grid,
        in_specs=placed,
        out_specs=(P(None, ALL, None), P()),
        check_vma=False,
    )
```

```python
import jax
import jax.numpy as jnp
from jax import lax
from jax.experimental import pallas as pl
from jax.experimental.pallas import tpu as pltpu
from jax.sharding import Mesh, PartitionSpec as P

F32 = jnp.float32
BF16 = jnp.bfloat16
ROW = ("y", "core")
COL = ("z", "x")
ALL = ("y", "core", "z", "x")
VMEM = pl.BlockSpec(memory_space=pltpu.VMEM)
SMEM = pl.BlockSpec(memory_space=pltpu.SMEM)
ANY = pl.BlockSpec(memory_space=pl.ANY)
MIB = 1024 * 1024


def sds(shape, dtype=F32):
    return jax.ShapeDtypeStruct(shape, dtype)


def split(v):
    hi = v.astype(BF16)
    lo = (v - hi.astype(F32)).astype(BF16)
    return hi, lo


def dot3(a, b, dims):
    (ah, al), (bh, bl) = a, b
    mm = lambda p, q: lax.dot_general(p, q, (dims, ((), ())), preferred_element_type=F32)
    return mm(ah, bh) + (mm(ah, bl) + mm(al, bh))


def pack_kernel(fb, w, out, sems):
    r = lax.axis_index("y") * 2 + lax.axis_index("core")
    z, x = lax.axis_index("z"), lax.axis_index("x")
    c = z * 4 + x
    part = 2 * x + z // 2
    row = pl.multiple_of(16 * (z % 2), 16)
    copies = []

    def start(src, dst):
        copy = pltpu.make_async_copy(src, dst, sems.at[len(copies)])
        copy.start()
        copies.append(copy)

    for f in range(2):
        own = [fb[f, 4 * r + i] for i in range(4)]
        piece = jnp.int32(0)
        for i in range(1, 4):
            piece = jnp.where((own[i] >> 2) == c, i, piece)
        for k in range(2):
            start(w.at[f, piece, k], out.at[:, k, 32 * f : 32 * f + 32])
        for d in range(8):
            named = jnp.int32(0)
            for i in range(1, 4):
                named = jnp.where((own[i] >> 3) == d, i, named)
            start(
                w.at[f, named, part // 4, part % 4, pl.ds(row, 16)],
                out.at[d // 2, d % 2, 64 + 16 * f : 80 + 16 * f],
            )
    for copy in copies:
        copy.wait()


def pick_kernel(tab, inc, slices, mine):
    for f in range(2):
        for t in range(2):
            p = tab[16 * f + 8 + t]
            v = inc[p >> 2, 32 * f : 32 * f + 32, :]
            for d in range(4):
                slices[d, 2 * f + t] = v
        for s in range(4):
            p = tab[16 * f + s]
            mine[4 * f + s] = inc[p >> 2, 64 + 16 * f : 80 + 16 * f, :]


def same_node(bounds, f):
    a = lax.broadcasted_iota(jnp.int32, (256, 256), 0)
    b = lax.broadcasted_iota(jnp.int32, (256, 256), 1)
    ia = jnp.zeros((256, 256), jnp.int32)
    ib = jnp.zeros((256, 256), jnp.int32)
    end = jnp.int32(0)
    for k in range(4):
        end = end + bounds[f, k]
        ia = ia + (a >= end).astype(jnp.int32)
        ib = ib + (b >= end).astype(jnp.int32)
    return ia == ib


def tile_kernel(fb, bounds, terms, inverse, hi, lo, tab, mask, base, tiles, sems):
    r = lax.axis_index("y") * 2 + lax.axis_index("core")
    c = lax.axis_index("z") * 4 + lax.axis_index("x")
    for k in range(32):
        tab[k] = 0
    copies = []
    for f in range(2):
        rows = jnp.int32(0)
        cols = jnp.int32(0)
        for p in range(32):
            b = fb[f, p]
            tab[16 * f + rows] = p
            rows = rows + ((b >> 3) == r).astype(jnp.int32)
            tab[16 * f + 8 + cols] = p
            cols = cols + ((b >> 2) == c).astype(jnp.int32)
        for s in range(4):
            for t in range(2):
                k = (4 * f + s) * 2 + t
                rb = fb[f, tab[16 * f + s]] & 7
                cb = fb[f, tab[16 * f + 8 + t]] & 3
                src = inverse.at[
                    pl.ds(pl.multiple_of(rb * 256, 256), 256),
                    pl.ds(pl.multiple_of(cb * 256, 256), 256),
                ]
                copy = pltpu.make_async_copy(src, tiles.at[k], sems.at[k])
                copy.start()
                copies.append(copy)
    for f in range(2):
        same = same_node(bounds, f)
        mask[f] = same.astype(F32)
        base[f] = jnp.where(same, terms[f], 0.0)
    for k in range(16):
        copies[k].wait()
        h, l = split(tiles[k])
        hi[k // 2, :, 256 * (k % 2) : 256 * (k % 2) + 256] = h
        lo[k // 2, :, 256 * (k % 2) : 256 * (k % 2) + 256] = l


def product_kernel(hi, lo, own, other, out, whole):
    core = lax.axis_index("core")
    for k in range(4):
        base = 256 * (k % 2)
        at = pl.multiple_of(base + 128 * core, 128)
        whole[k // 2, pl.ds(at, 128), :] = own[:, k].reshape(128, 256)
        at = pl.multiple_of(base + 128 * (1 - core), 128)
        whole[k // 2, pl.ds(at, 128), :] = other[:, k].reshape(128, 256)
    for f in range(2):
        w = split(whole[f])
        for s in range(4):
            total = dot3((hi[4 * f + s], lo[4 * f + s]), w, ((1,), (0,)))
            for d in range(16):
                at = 64 * (d % 4) + 16 * (d // 4)
                out[d, 4 * f + s] = total[at : at + 16, :]


def reduce_kernel(tab, mask, parts, mine, keep, send):
    core = lax.axis_index("core")
    for ref in (keep, send):
        for d in range(4):
            ref[d, 0:32] = jnp.zeros((32, 256), F32)
    for f in range(2):
        rows = []
        for s in range(4):
            v = parts[0, 4 * f + s]
            for d in range(1, 16):
                v = v + parts[d, 4 * f + s]
            rows.append(v)
            owner = tab[16 * f + s] >> 2

            @pl.when((owner & 1) == core)
            def _():
                keep[owner >> 1, 16 * f : 16 * f + 16] = -v

            @pl.when((owner & 1) != core)
            def _():
                send[owner >> 1, 16 * f : 16 * f + 16] = -v

        left = mine[4 * f : 4 * f + 4].reshape(64, 256)
        right = jnp.concatenate(rows, axis=0)
        full = dot3(split(left), split(right), ((0,), (0,)))
        full = full * mask[f]
        packed = full[:, :128] + full[:, 128:]
        chunks = []
        for d in range(4):
            part = packed[64 * d : 64 * d + 64]
            chunks.append(jnp.concatenate([part[:32], part[32:]], axis=1))

        @pl.when(core == f)
        def _():
            for d in range(4):
                keep[d, 32:64] = chunks[d]

        @pl.when(core != f)
        def _():
            for d in range(4):
                send[d, 32:64] = chunks[d]


def join_kernel(keep, got, out):
    for d in range(4):
        out[d, 0:32] = keep[d, 0:32]
        out[d, 32:64] = got[d, 0:32]
        out[d, 64:96] = keep[d, 32:64] + got[d, 32:64]


def place_kernel(fb, inc, out):
    core = lax.axis_index("core")
    r = lax.axis_index("y") * 2 + core
    total = (inc[0, 64:96] + inc[1, 64:96]) + (inc[2, 64:96] + inc[3, 64:96])
    for d in range(4):
        out[d, 32:64] = total
    for f in range(2):
        for i in range(4):
            source = fb[f, 4 * r + i] >> 3
            at = pl.multiple_of(32 * ((source & 1) ^ core) + 16 * f, 16)
            out[i, 16 * f : 16 * f + 16] = inc[source >> 1, pl.ds(at, 16), :]


def border_kernel(inc, border, out):
    for z in range(4):
        for f in range(2):
            border[f, 16 * z : 16 * z + 16] = inc[z, 16 * f : 16 * f + 16, :]
    total = (inc[0, 32:64] + inc[1, 32:64]) + (inc[2, 32:64] + inc[3, 32:64])
    for d in range(16):
        out[d] = total


def chunk_kernel(inc, out):
    for y in range(4):
        at = 4 * y
        out[y] = (inc[at] + inc[at + 1]) + (inc[at + 2] + inc[at + 3])


def finish_kernel(own, other, mask, base, out):
    core = lax.axis_index("core")
    for rel, chunks in enumerate((own, other)):
        f = core ^ rel
        for d in range(4):
            v = chunks[d]
            v = jnp.concatenate([v[:, :128], v[:, 128:]], axis=0)
            at = slice(64 * d, 64 * d + 64)
            out[f, at] = base[f, at] + mask[f, at] * jnp.concatenate([v, v], axis=1)


def call(kernel, ins, out_shape, out_specs=None, scratch=(), limit=8, cost=None):
    if out_specs is None:
        out_specs = jax.tree.map(lambda _: VMEM, out_shape)
    return pl.pallas_call(
        kernel,
        in_specs=ins,
        out_shape=out_shape,
        out_specs=out_specs,
        scratch_shapes=scratch,
        cost_estimate=cost,
        compiler_params=pltpu.CompilerParams(vmem_limit_bytes=limit * MIB),
    )


def a2a(v, axes):
    return lax.all_to_all(v, axes, 0, 0, tiled=True)


def hbm(v):
    return pltpu.with_memory_space_constraint(v, pltpu.HBM)


def swap(v):
    return lax.ppermute(v, "core", [(0, 1), (1, 0)])


def body(inverse, fb, panels, terms, bounds):
    outgoing = call(
        pack_kernel,
        [SMEM, ANY],
        sds((4, 2, 96, 256)),
        scratch=[pltpu.SemaphoreType.DMA((20,))],
    )(hbm(fb), hbm(panels.reshape(2, 4, 2, 4, 32, 256)))
    incoming = a2a(outgoing.reshape(8, 96, 256), ROW)
    hi, lo, tab, mask, base = call(
        tile_kernel,
        [SMEM, SMEM, VMEM, ANY],
        (
            sds((8, 256, 512), BF16),
            sds((8, 256, 512), BF16),
            sds((32,), jnp.int32),
            sds((2, 256, 256)),
            sds((2, 256, 256)),
        ),
        (VMEM, VMEM, SMEM, VMEM, VMEM),
        scratch=[pltpu.VMEM((16, 256, 256), F32), pltpu.SemaphoreType.DMA((16,))],
        limit=16,
        cost=pl.CostEstimate(flops=4 * MIB, bytes_accessed=12 * MIB, transcendentals=0),
    )(fb, bounds, terms, hbm(inverse))
    slices, mine = call(
        pick_kernel, [SMEM, VMEM], (sds((4, 4, 32, 256)), sds((8, 16, 256)))
    )(tab, incoming)
    own = a2a(slices, "y")
    other = swap(own)
    parts = call(
        product_kernel,
        [VMEM, VMEM, VMEM, VMEM],
        sds((16, 8, 16, 256)),
        scratch=[pltpu.VMEM((2, 512, 256), F32)],
        limit=16,
    )(hi, lo, own, other)
    parts = a2a(parts, COL)
    keep, send = call(
        reduce_kernel, [SMEM, VMEM, VMEM, VMEM], (sds((4, 64, 256)), sds((4, 64, 256)))
    )(tab, mask, parts, mine)
    v = call(join_kernel, [VMEM, VMEM], sds((4, 96, 256)))(keep, swap(send))
    v = a2a(v, "y")
    v = call(place_kernel, [SMEM, VMEM], sds((4, 64, 256)))(fb, v)
    v = a2a(v, "z")
    border, v = call(border_kernel, [VMEM], (sds((2, 64, 256)), sds((16, 32, 256))))(v)
    v = a2a(v, ("y", "x"))
    own = call(chunk_kernel, [VMEM], sds((4, 32, 256)))(v)
    other = swap(own)
    diag = call(
        finish_kernel,
        [VMEM, VMEM, VMEM, VMEM],
        sds((2, 256, 256)),
    )(own, other, mask, base)
    return border, diag


def solution(mesh):
    grid = Mesh(mesh.devices.reshape(4, 2, 4, 4), ALL)
    placed = (P(ROW, COL), P(), P(None, ROW, None), P(), P())
    return jax.shard_map(
        body,
        mesh=grid,
        in_specs=placed,
        out_specs=(P(None, ALL, None), P()),
        check_vma=False,
    )
```

```python
import jax
import jax.numpy as jnp
from jax import lax
from jax.experimental import pallas as pl
from jax.experimental.pallas import tpu as pltpu
from jax.sharding import Mesh, PartitionSpec as P

F32 = jnp.float32
BF16 = jnp.bfloat16
ROW = ("y", "core")
COL = ("z", "x")
ALL = ("y", "core", "z", "x")
VMEM = pl.BlockSpec(memory_space=pltpu.VMEM)
SMEM = pl.BlockSpec(memory_space=pltpu.SMEM)
ANY = pl.BlockSpec(memory_space=pl.ANY)
MIB = 1024 * 1024


def sds(shape, dtype=F32):
    return jax.ShapeDtypeStruct(shape, dtype)


def split(v):
    hi = v.astype(BF16)
    lo = (v - hi.astype(F32)).astype(BF16)
    return hi, lo


def dot3(a, b, dims):
    (ah, al), (bh, bl) = a, b
    mm = lambda p, q: lax.dot_general(p, q, (dims, ((), ())), preferred_element_type=F32)
    return mm(ah, bh) + (mm(ah, bl) + mm(al, bh))


def pack_kernel(fb, w, out, sems):
    r = lax.axis_index("y") * 2 + lax.axis_index("core")
    z, x = lax.axis_index("z"), lax.axis_index("x")
    c = z * 4 + x
    part = 2 * x + z // 2
    row = pl.multiple_of(16 * (z % 2), 16)
    copies = []

    def start(src, dst):
        copy = pltpu.make_async_copy(src, dst, sems.at[len(copies)])
        copy.start()
        copies.append(copy)

    for f in range(2):
        own = [fb[f, 4 * r + i] for i in range(4)]
        piece = jnp.int32(0)
        for i in range(1, 4):
            piece = jnp.where((own[i] >> 2) == c, i, piece)
        for k in range(2):
            start(w.at[f, piece, k], out.at[:, k, 32 * f : 32 * f + 32])
        for d in range(8):
            named = jnp.int32(0)
            for i in range(1, 4):
                named = jnp.where((own[i] >> 3) == d, i, named)
            start(
                w.at[f, named, part // 4, part % 4, pl.ds(row, 16)],
                out.at[d // 2, d % 2, 64 + 16 * f : 80 + 16 * f],
            )
    for copy in copies:
        copy.wait()


def pick_kernel(tab, inc, slices, mine):
    for f in range(2):
        for t in range(2):
            p = tab[16 * f + 8 + t]
            v = inc[p >> 2, 32 * f : 32 * f + 32, :]
            for d in range(4):
                slices[d, 2 * f + t] = v
        for s in range(4):
            p = tab[16 * f + s]
            mine[4 * f + s] = inc[p >> 2, 64 + 16 * f : 80 + 16 * f, :]


def same_node(bounds, f):
    a = lax.broadcasted_iota(jnp.int32, (256, 256), 0)
    b = lax.broadcasted_iota(jnp.int32, (256, 256), 1)
    ia = jnp.zeros((256, 256), jnp.int32)
    ib = jnp.zeros((256, 256), jnp.int32)
    end = jnp.int32(0)
    for k in range(4):
        end = end + bounds[f, k]
        ia = ia + (a >= end).astype(jnp.int32)
        ib = ib + (b >= end).astype(jnp.int32)
    return ia == ib


def tile_kernel(fb, bounds, terms, inverse, hi, lo, tab, mask, base, tiles, sems):
    r = lax.axis_index("y") * 2 + lax.axis_index("core")
    c = lax.axis_index("z") * 4 + lax.axis_index("x")
    for k in range(32):
        tab[k] = 0
    copies = []
    for f in range(2):
        rows = jnp.int32(0)
        cols = jnp.int32(0)
        for p in range(32):
            b = fb[f, p]
            tab[16 * f + rows] = p
            rows = rows + ((b >> 3) == r).astype(jnp.int32)
            tab[16 * f + 8 + cols] = p
            cols = cols + ((b >> 2) == c).astype(jnp.int32)
        for s in range(4):
            for t in range(2):
                k = (4 * f + s) * 2 + t
                rb = fb[f, tab[16 * f + s]] & 7
                cb = fb[f, tab[16 * f + 8 + t]] & 3
                src = inverse.at[
                    pl.ds(pl.multiple_of(rb * 256, 256), 256),
                    pl.ds(pl.multiple_of(cb * 256, 256), 256),
                ]
                copy = pltpu.make_async_copy(src, tiles.at[k], sems.at[k])
                copy.start()
                copies.append(copy)
    for f in range(2):
        same = same_node(bounds, f)
        mask[f] = same.astype(F32)
        base[f] = jnp.where(same, terms[f], 0.0)
    for k in range(16):
        copies[k].wait()
        h, l = split(tiles[k])
        hi[k // 2, :, 256 * (k % 2) : 256 * (k % 2) + 256] = h
        lo[k // 2, :, 256 * (k % 2) : 256 * (k % 2) + 256] = l


def product_kernel(hi, lo, own, other, out, whole, high, sems):
    core = lax.axis_index("core")
    copies = []
    for k in range(8):
        copy = pltpu.make_async_copy(hi.at[k], high.at[k], sems.at[k])
        copy.start()
        copies.append(copy)
    for k in range(4):
        base = 256 * (k % 2)
        at = pl.multiple_of(base + 128 * core, 128)
        whole[k // 2, pl.ds(at, 128), :] = own[:, k].reshape(128, 256)
        at = pl.multiple_of(base + 128 * (1 - core), 128)
        whole[k // 2, pl.ds(at, 128), :] = other[:, k].reshape(128, 256)
    for f in range(2):
        w = split(whole[f])
        for s in range(4):
            copies[4 * f + s].wait()
            total = dot3((high[4 * f + s], lo[4 * f + s]), w, ((1,), (0,)))
            for x in range(4):
                for z in range(4):
                    at = 64 * x + 16 * z
                    first = jnp.where(core == 0, x, z)
                    second = jnp.where(core == 0, z, x)
                    out[first, second, 4 * f + s] = total[at : at + 16, :]


def half_kernel(inc, out):
    for d in range(4):
        for k in range(8):
            out[d, k] = (inc[0, d, k] + inc[1, d, k]) + (inc[2, d, k] + inc[3, d, k])


def reduce_kernel(tab, mask, parts, mine, out):
    for d in range(8):
        out[d, 0:32] = jnp.zeros((32, 256), F32)
    for f in range(2):
        rows = []
        for s in range(4):
            k = 4 * f + s
            v = (parts[0, k] + parts[1, k]) + (parts[2, k] + parts[3, k])
            rows.append(v)
            out[tab[16 * f + s] >> 2, 16 * f : 16 * f + 16] = -v
        left = mine[4 * f : 4 * f + 4].reshape(64, 256)
        right = jnp.concatenate(rows, axis=0)
        full = dot3(split(left), split(right), ((0,), (0,)))
        full = full * mask[f]
        packed = full[:, :128] + full[:, 128:]
        for d in range(4):
            part = packed[64 * d : 64 * d + 64]
            out[4 * f + d, 32:64] = jnp.concatenate([part[:32], part[32:]], axis=1)


def place_kernel(fb, inc, out):
    r = lax.axis_index("y") * 2 + lax.axis_index("core")
    total = inc[0, 32:64]
    for d in range(1, 8):
        total = total + inc[d, 32:64]
    for d in range(4):
        out[d, 32:64] = total
    for f in range(2):
        for i in range(4):
            out[i, 16 * f : 16 * f + 16] = inc[fb[f, 4 * r + i] >> 3, 16 * f : 16 * f + 16, :]


def border_kernel(inc, border, out):
    for z in range(4):
        for f in range(2):
            border[f, 16 * z : 16 * z + 16] = inc[z, 16 * f : 16 * f + 16, :]
    total = (inc[0, 32:64] + inc[1, 32:64]) + (inc[2, 32:64] + inc[3, 32:64])
    for d in range(16):
        out[d] = total


def chunk_kernel(inc, out):
    for y in range(4):
        at = 4 * y
        out[y] = (inc[at] + inc[at + 1]) + (inc[at + 2] + inc[at + 3])


def finish_kernel(own, other, mask, base, out, chunks):
    core = lax.axis_index("core")
    for y in range(4):
        chunks[2 * y + core] = own[y]
        chunks[2 * y + 1 - core] = other[y]
    for f in range(2):
        for d in range(4):
            v = chunks[4 * f + d]
            v = jnp.concatenate([v[:, :128], v[:, 128:]], axis=0)
            at = slice(64 * d, 64 * d + 64)
            out[f, at] = base[f, at] + mask[f, at] * jnp.concatenate([v, v], axis=1)


def call(kernel, ins, out_shape, out_specs=None, scratch=(), limit=8, cost=None):
    if out_specs is None:
        out_specs = jax.tree.map(lambda _: VMEM, out_shape)
    return pl.pallas_call(
        kernel,
        in_specs=ins,
        out_shape=out_shape,
        out_specs=out_specs,
        scratch_shapes=scratch,
        cost_estimate=cost,
        compiler_params=pltpu.CompilerParams(vmem_limit_bytes=limit * MIB),
    )


def a2a(v, axes):
    return lax.all_to_all(v, axes, 0, 0, tiled=True)


def grouped(v, stage):
    groups = []
    for line in range(8):
        for o in range(4):
            along_x = [16 * line + 4 * o + i for i in range(4)]
            along_z = [16 * line + 4 * i + o for i in range(4)]
            groups.append(along_x if line % 2 == stage else along_z)
    return lax.all_to_all(v, ALL, 0, 0, tiled=True, axis_index_groups=groups)


def hbm(v):
    return pltpu.with_memory_space_constraint(v, pltpu.HBM)


def swap(v):
    return lax.ppermute(v, "core", [(0, 1), (1, 0)])


def body(inverse, fb, panels, terms, bounds):
    outgoing = call(
        pack_kernel,
        [SMEM, ANY],
        sds((4, 2, 96, 256)),
        ANY,
        scratch=[pltpu.SemaphoreType.DMA((20,))],
    )(hbm(fb), hbm(panels.reshape(2, 4, 2, 4, 32, 256)))
    incoming = a2a(outgoing.reshape(8, 96, 256), ROW)
    hi, lo, tab, mask, base = call(
        tile_kernel,
        [SMEM, SMEM, VMEM, ANY],
        (
            sds((8, 256, 512), BF16),
            sds((8, 256, 512), BF16),
            sds((32,), jnp.int32),
            sds((2, 256, 256)),
            sds((2, 256, 256)),
        ),
        (VMEM, VMEM, SMEM, VMEM, VMEM),
        scratch=[pltpu.VMEM((16, 256, 256), F32), pltpu.SemaphoreType.DMA((16,))],
        limit=16,
        cost=pl.CostEstimate(flops=4 * MIB, bytes_accessed=12 * MIB, transcendentals=0),
    )(fb, bounds, terms, hbm(inverse))
    slices, mine = call(
        pick_kernel, [SMEM, VMEM], (sds((4, 4, 32, 256)), sds((8, 16, 256)))
    )(tab, incoming)
    own = a2a(slices, "y")
    other = swap(own)
    parts = call(
        product_kernel,
        [ANY, VMEM, VMEM, VMEM],
        sds((4, 4, 8, 16, 256)),
        scratch=[
            pltpu.VMEM((2, 512, 256), F32),
            pltpu.VMEM((8, 256, 512), BF16),
            pltpu.SemaphoreType.DMA((8,)),
        ],
        limit=16,
    )(hbm(hi), lo, own, other)
    parts = grouped(parts, 0)
    parts = call(half_kernel, [VMEM], sds((4, 8, 16, 256)))(parts)
    parts = grouped(parts, 1)
    v = call(reduce_kernel, [SMEM, VMEM, VMEM, VMEM], sds((8, 64, 256)))(tab, mask, parts, mine)
    v = a2a(v, ROW)
    v = call(place_kernel, [SMEM, VMEM], sds((4, 64, 256)))(fb, v)
    v = a2a(v, "z")
    border, v = call(border_kernel, [VMEM], (sds((2, 64, 256)), sds((16, 32, 256))))(v)
    v = a2a(v, ("y", "x"))
    own = call(chunk_kernel, [VMEM], sds((4, 32, 256)))(v)
    other = swap(own)
    diag = call(
        finish_kernel,
        [VMEM, VMEM, VMEM, VMEM],
        sds((2, 256, 256)),
        scratch=[pltpu.VMEM((8, 32, 256), F32)],
    )(own, other, mask, base)
    return border, diag


def solution(mesh):
    grid = Mesh(mesh.devices.reshape(4, 2, 4, 4), ALL)
    placed = (P(ROW, COL), P(), P(None, ROW, None), P(), P())
    return jax.shard_map(
        body,
        mesh=grid,
        in_specs=placed,
        out_specs=(P(None, ALL, None), P()),
        check_vma=False,
    )
```

```python
import jax
import jax.numpy as jnp
from jax import lax
from jax.experimental import pallas as pl
from jax.experimental.pallas import tpu as pltpu
from jax.sharding import Mesh, PartitionSpec as P

F32 = jnp.float32
BF16 = jnp.bfloat16
ROW = ("y", "core")
COL = ("z", "x")
ALL = ("y", "core", "z", "x")
VMEM = pl.BlockSpec(memory_space=pltpu.VMEM)
SMEM = pl.BlockSpec(memory_space=pltpu.SMEM)
ANY = pl.BlockSpec(memory_space=pl.ANY)
MIB = 1024 * 1024


def sds(shape, dtype=F32):
    return jax.ShapeDtypeStruct(shape, dtype)


def split(v):
    hi = v.astype(BF16)
    lo = (v - hi.astype(F32)).astype(BF16)
    return hi, lo


def dot3(a, b, dims):
    (ah, al), (bh, bl) = a, b
    mm = lambda p, q: lax.dot_general(p, q, (dims, ((), ())), preferred_element_type=F32)
    return mm(ah, bh) + (mm(ah, bl) + mm(al, bh))


def pack_kernel(fb, w, out, sems):
    r = lax.axis_index("y") * 2 + lax.axis_index("core")
    z, x = lax.axis_index("z"), lax.axis_index("x")
    c = z * 4 + x
    part = 2 * x + z // 2
    row = pl.multiple_of(16 * (z % 2), 16)
    copies = []

    def start(src, dst):
        copy = pltpu.make_async_copy(src, dst, sems.at[len(copies)])
        copy.start()
        copies.append(copy)

    for f in range(2):
        own = [fb[f, 4 * r + i] for i in range(4)]
        piece = jnp.int32(0)
        for i in range(1, 4):
            piece = jnp.where((own[i] >> 2) == c, i, piece)
        for k in range(2):
            start(w.at[f, piece, k], out.at[:, k, 32 * f : 32 * f + 32])
        for d in range(8):
            named = jnp.int32(0)
            for i in range(1, 4):
                named = jnp.where((own[i] >> 3) == d, i, named)
            start(
                w.at[f, named, part // 4, part % 4, pl.ds(row, 16)],
                out.at[d // 2, d % 2, 64 + 16 * f : 80 + 16 * f],
            )
    for copy in copies:
        copy.wait()


def pick_kernel(tab, inc, slices, mine):
    for f in range(2):
        for t in range(2):
            p = tab[16 * f + 8 + t]
            v = inc[p >> 2, 32 * f : 32 * f + 32, :]
            for d in range(4):
                slices[d, 2 * f + t] = v
        for s in range(4):
            p = tab[16 * f + s]
            mine[4 * f + s] = inc[p >> 2, 64 + 16 * f : 80 + 16 * f, :]


def same_node(bounds, f):
    a = lax.broadcasted_iota(jnp.int32, (256, 256), 0)
    b = lax.broadcasted_iota(jnp.int32, (256, 256), 1)
    ia = jnp.zeros((256, 256), jnp.int32)
    ib = jnp.zeros((256, 256), jnp.int32)
    end = jnp.int32(0)
    for k in range(4):
        end = end + bounds[f, k]
        ia = ia + (a >= end).astype(jnp.int32)
        ib = ib + (b >= end).astype(jnp.int32)
    return ia == ib


def fetch_tiles(f, fb, tab, inverse, hi, lo, tiles, sems):
    copies = []
    for s in range(4):
        for t in range(2):
            k = 2 * s + t
            rb = fb[f, tab[16 * f + s]] & 7
            cb = fb[f, tab[16 * f + 8 + t]] & 3
            src = inverse.at[
                pl.ds(pl.multiple_of(rb * 256, 256), 256),
                pl.ds(pl.multiple_of(cb * 256, 256), 256),
            ]
            copy = pltpu.make_async_copy(src, tiles.at[k], sems.at[k])
            copy.start()
            copies.append(copy)
    for k in range(8):
        copies[k].wait()
        h, l = split(tiles[k])
        hi[k // 2, :, 256 * (k % 2) : 256 * (k % 2) + 256] = h
        lo[k // 2, :, 256 * (k % 2) : 256 * (k % 2) + 256] = l


def first_kernel(fb, bounds, inverse, hi, lo, tab, mask, tiles, sems):
    r = lax.axis_index("y") * 2 + lax.axis_index("core")
    c = lax.axis_index("z") * 4 + lax.axis_index("x")
    for k in range(32):
        tab[k] = 0
    for f in range(2):
        rows = jnp.int32(0)
        cols = jnp.int32(0)
        for p in range(32):
            b = fb[f, p]
            tab[16 * f + rows] = p
            rows = rows + ((b >> 3) == r).astype(jnp.int32)
            tab[16 * f + 8 + cols] = p
            cols = cols + ((b >> 2) == c).astype(jnp.int32)
    for f in range(2):
        mask[f] = same_node(bounds, f).astype(F32)
    fetch_tiles(0, fb, tab, inverse, hi, lo, tiles, sems)


def second_kernel(fb, tab, inverse, after, hi, lo, tiles, sems):
    fetch_tiles(1, fb, tab, inverse, hi, lo, tiles, sems)


def product_kernel(hi0, lo0, hi1, lo1, own, other, out, whole):
    core = lax.axis_index("core")
    for k in range(4):
        base = 256 * (k % 2)
        at = pl.multiple_of(base + 128 * core, 128)
        whole[k // 2, pl.ds(at, 128), :] = own[:, k].reshape(128, 256)
        at = pl.multiple_of(base + 128 * (1 - core), 128)
        whole[k // 2, pl.ds(at, 128), :] = other[:, k].reshape(128, 256)
    for f in range(2):
        w = split(whole[f])
        hi, lo = ((hi0, lo0), (hi1, lo1))[f]
        for s in range(4):
            total = dot3((hi[s], lo[s]), w, ((1,), (0,)))
            for x in range(4):
                for z in range(4):
                    at = 64 * x + 16 * z
                    first = jnp.where(core == 0, x, z)
                    second = jnp.where(core == 0, z, x)
                    out[first, second, 4 * f + s] = total[at : at + 16, :]


def half_kernel(inc, out):
    for d in range(4):
        for k in range(8):
            out[d, k] = (inc[0, d, k] + inc[1, d, k]) + (inc[2, d, k] + inc[3, d, k])


def reduce_kernel(tab, mask, parts, mine, out):
    for d in range(8):
        out[d, 0:32] = jnp.zeros((32, 256), F32)
    for f in range(2):
        rows = []
        for s in range(4):
            k = 4 * f + s
            v = (parts[0, k] + parts[1, k]) + (parts[2, k] + parts[3, k])
            rows.append(v)
            out[tab[16 * f + s] >> 2, 16 * f : 16 * f + 16] = -v
        left = mine[4 * f : 4 * f + 4].reshape(64, 256)
        right = jnp.concatenate(rows, axis=0)
        full = dot3(split(left), split(right), ((0,), (0,)))
        full = full * mask[f]
        packed = full[:, :128] + full[:, 128:]
        for d in range(4):
            part = packed[64 * d : 64 * d + 64]
            out[4 * f + d, 32:64] = jnp.concatenate([part[:32], part[32:]], axis=1)


def place_kernel(fb, inc, out):
    r = lax.axis_index("y") * 2 + lax.axis_index("core")
    total = inc[0, 32:64]
    for d in range(1, 8):
        total = total + inc[d, 32:64]
    for d in range(4):
        out[d, 32:64] = total
    for f in range(2):
        for i in range(4):
            out[i, 16 * f : 16 * f + 16] = inc[fb[f, 4 * r + i] >> 3, 16 * f : 16 * f + 16, :]


def border_kernel(inc, border, out):
    for z in range(4):
        for f in range(2):
            border[f, 16 * z : 16 * z + 16] = inc[z, 16 * f : 16 * f + 16, :]
    total = (inc[0, 32:64] + inc[1, 32:64]) + (inc[2, 32:64] + inc[3, 32:64])
    for d in range(16):
        out[d] = total


def chunk_kernel(inc, out):
    for y in range(4):
        at = 4 * y
        out[y] = (inc[at] + inc[at + 1]) + (inc[at + 2] + inc[at + 3])


def finish_kernel(own, other, mask, terms, out, chunks):
    core = lax.axis_index("core")
    for y in range(4):
        chunks[2 * y + core] = own[y]
        chunks[2 * y + 1 - core] = other[y]
    for f in range(2):
        for d in range(4):
            v = chunks[4 * f + d]
            v = jnp.concatenate([v[:, :128], v[:, 128:]], axis=0)
            at = slice(64 * d, 64 * d + 64)
            out[f, at] = mask[f, at] * (terms[f, at] + jnp.concatenate([v, v], axis=1))


def call(kernel, ins, out_shape, out_specs=None, scratch=(), limit=8, cost=None):
    if out_specs is None:
        out_specs = jax.tree.map(lambda _: VMEM, out_shape)
    return pl.pallas_call(
        kernel,
        in_specs=ins,
        out_shape=out_shape,
        out_specs=out_specs,
        scratch_shapes=scratch,
        cost_estimate=cost,
        compiler_params=pltpu.CompilerParams(vmem_limit_bytes=limit * MIB),
    )


def a2a(v, axes):
    return lax.all_to_all(v, axes, 0, 0, tiled=True)


def grouped(v, stage):
    groups = []
    for line in range(8):
        for o in range(4):
            along_x = [16 * line + 4 * o + i for i in range(4)]
            along_z = [16 * line + 4 * i + o for i in range(4)]
            groups.append(along_x if line % 2 == stage else along_z)
    return lax.all_to_all(v, ALL, 0, 0, tiled=True, axis_index_groups=groups)


def hbm(v):
    return pltpu.with_memory_space_constraint(v, pltpu.HBM)


def swap(v):
    return lax.ppermute(v, "core", [(0, 1), (1, 0)])


def body(inverse, fb, panels, terms, bounds):
    outgoing = call(
        pack_kernel,
        [SMEM, ANY],
        sds((4, 2, 96, 256)),
        scratch=[pltpu.SemaphoreType.DMA((20,))],
    )(hbm(fb), hbm(panels.reshape(2, 4, 2, 4, 32, 256)))
    incoming = a2a(outgoing.reshape(8, 96, 256), ROW)
    tiles = (sds((4, 256, 512), BF16), sds((4, 256, 512), BF16))
    buffers = [pltpu.VMEM((8, 256, 256), F32), pltpu.SemaphoreType.DMA((8,))]
    cost = pl.CostEstimate(flops=2 * MIB, bytes_accessed=6 * MIB, transcendentals=0)
    hi0, lo0, tab, mask = call(
        first_kernel,
        [SMEM, SMEM, ANY],
        (*tiles, sds((32,), jnp.int32), sds((2, 256, 256))),
        (VMEM, VMEM, SMEM, VMEM),
        scratch=buffers,
        limit=16,
        cost=cost,
    )(fb, bounds, hbm(inverse))
    slices, mine = call(
        pick_kernel, [SMEM, VMEM], (sds((4, 4, 32, 256)), sds((8, 16, 256)))
    )(tab, incoming)
    own = a2a(slices, "y")
    other = swap(own)
    hi1, lo1 = call(
        second_kernel, [SMEM, SMEM, ANY, ANY], tiles, scratch=buffers, limit=16, cost=cost
    )(fb, tab, hbm(inverse), own)
    parts = call(
        product_kernel,
        [VMEM] * 6,
        sds((4, 4, 8, 16, 256)),
        scratch=[pltpu.VMEM((2, 512, 256), F32)],
        limit=16,
    )(hi0, lo0, hi1, lo1, own, other)
    parts = grouped(parts, 0)
    parts = call(half_kernel, [VMEM], sds((4, 8, 16, 256)))(parts)
    parts = grouped(parts, 1)
    v = call(reduce_kernel, [SMEM, VMEM, VMEM, VMEM], sds((8, 64, 256)))(tab, mask, parts, mine)
    v = a2a(v, ROW)
    v = call(place_kernel, [SMEM, VMEM], sds((4, 64, 256)))(fb, v)
    v = a2a(v, "z")
    border, v = call(border_kernel, [VMEM], (sds((2, 64, 256)), sds((16, 32, 256))))(v)
    v = a2a(v, ("y", "x"))
    own = call(chunk_kernel, [VMEM], sds((4, 32, 256)))(v)
    other = swap(own)
    diag = call(
        finish_kernel,
        [VMEM, VMEM, VMEM, VMEM],
        sds((2, 256, 256)),
        scratch=[pltpu.VMEM((8, 32, 256), F32)],
    )(own, other, mask, terms)
    return border, diag


def solution(mesh):
    grid = Mesh(mesh.devices.reshape(4, 2, 4, 4), ALL)
    placed = (P(ROW, COL), P(), P(None, ROW, None), P(), P())
    return jax.shard_map(
        body,
        mesh=grid,
        in_specs=placed,
        out_specs=(P(None, ALL, None), P()),
        check_vma=False,
    )
```

```python
import jax
import jax.numpy as jnp
from jax import lax
from jax.experimental import pallas as pl
from jax.experimental.pallas import tpu as pltpu
from jax.sharding import Mesh, PartitionSpec as P

F32 = jnp.float32
BF16 = jnp.bfloat16
ROW = ("y", "core")
COL = ("z", "x")
ALL = ("y", "core", "z", "x")
VMEM = pl.BlockSpec(memory_space=pltpu.VMEM)
SMEM = pl.BlockSpec(memory_space=pltpu.SMEM)
ANY = pl.BlockSpec(memory_space=pl.ANY)
MIB = 1024 * 1024


def sds(shape, dtype=F32):
    return jax.ShapeDtypeStruct(shape, dtype)


def split(v):
    hi = v.astype(BF16)
    lo = (v - hi.astype(F32)).astype(BF16)
    return hi, lo


def dot3(a, b, dims):
    (ah, al), (bh, bl) = a, b
    mm = lambda p, q: lax.dot_general(p, q, (dims, ((), ())), preferred_element_type=F32)
    return mm(ah, bh) + (mm(ah, bl) + mm(al, bh))


def pack_kernel(fb, w, out, stage, ins, outs):
    r = lax.axis_index("y") * 2 + lax.axis_index("core")
    z, x = lax.axis_index("z"), lax.axis_index("x")
    c = z * 4 + x
    part = 2 * x + z // 2
    row = pl.multiple_of(16 * (z % 2), 16)
    pieces, mine = [], []
    for f in range(2):
        own = [fb[f, 4 * r + i] for i in range(4)]
        piece = jnp.int32(0)
        for i in range(1, 4):
            piece = jnp.where((own[i] >> 2) == c, i, piece)
        at = (slice(None), slice(32 * f, 32 * f + 32))
        copy = pltpu.make_async_copy(w.at[f, piece], stage.at[at], ins.at[f])
        copy.start()
        pieces.append((copy, pltpu.make_async_copy(stage.at[at], out.at[at], outs.at[f])))
    for f in range(2):
        own = [fb[f, 4 * r + i] for i in range(4)]
        for d in range(8):
            named = jnp.int32(0)
            for i in range(1, 4):
                named = jnp.where((own[i] >> 3) == d, i, named)
            copy = pltpu.make_async_copy(
                w.at[f, named, part, pl.ds(row, 16)],
                stage.at[d, 64 + 16 * f : 80 + 16 * f],
                ins.at[2 + 8 * f + d],
            )
            copy.start()
            mine.append(copy)
    for first, second in pieces:
        first.wait()
        second.start()
    for copy in mine:
        copy.wait()
    at = (slice(None), slice(64, 96))
    last = pltpu.make_async_copy(stage.at[at], out.at[at], outs.at[2])
    last.start()
    for first, second in pieces:
        second.wait()
    last.wait()


def pick_kernel(tab, inc, slices, mine):
    for f in range(2):
        for t in range(2):
            p = tab[16 * f + 8 + t]
            v = inc[p >> 2, 32 * f : 32 * f + 32, :]
            for d in range(4):
                slices[d, 2 * f + t] = v
        for s in range(4):
            p = tab[16 * f + s]
            mine[4 * f + s] = inc[p >> 2, 64 + 16 * f : 80 + 16 * f, :]


def same_node(bounds, f):
    a = lax.broadcasted_iota(jnp.int32, (256, 256), 0)
    b = lax.broadcasted_iota(jnp.int32, (256, 256), 1)
    ia = jnp.zeros((256, 256), jnp.int32)
    ib = jnp.zeros((256, 256), jnp.int32)
    end = jnp.int32(0)
    for k in range(4):
        end = end + bounds[f, k]
        ia = ia + (a >= end).astype(jnp.int32)
        ib = ib + (b >= end).astype(jnp.int32)
    return ia == ib


def fetch_tiles(f, fb, tab, inverse, hi, lo, tiles, sems):
    copies = []
    for s in range(4):
        for t in range(2):
            k = 2 * s + t
            rb = fb[f, tab[16 * f + s]] & 7
            cb = fb[f, tab[16 * f + 8 + t]] & 3
            src = inverse.at[
                pl.ds(pl.multiple_of(rb * 256, 256), 256),
                pl.ds(pl.multiple_of(cb * 256, 256), 256),
            ]
            copy = pltpu.make_async_copy(src, tiles.at[k], sems.at[k])
            copy.start()
            copies.append(copy)
    for k in range(8):
        copies[k].wait()
        h, l = split(tiles[k])
        hi[k // 2, :, 256 * (k % 2) : 256 * (k % 2) + 256] = h
        lo[k // 2, :, 256 * (k % 2) : 256 * (k % 2) + 256] = l


def first_kernel(fb, bounds, inverse, hi, lo, tab, mask, tiles, sems):
    r = lax.axis_index("y") * 2 + lax.axis_index("core")
    c = lax.axis_index("z") * 4 + lax.axis_index("x")
    for k in range(32):
        tab[k] = 0
    for f in range(2):
        rows = jnp.int32(0)
        cols = jnp.int32(0)
        for p in range(32):
            b = fb[f, p]
            tab[16 * f + rows] = p
            rows = rows + ((b >> 3) == r).astype(jnp.int32)
            tab[16 * f + 8 + cols] = p
            cols = cols + ((b >> 2) == c).astype(jnp.int32)
    for f in range(2):
        mask[f] = same_node(bounds, f).astype(F32)
    fetch_tiles(0, fb, tab, inverse, hi, lo, tiles, sems)


def second_kernel(fb, tab, inverse, after, hi, lo, tiles, sems):
    fetch_tiles(1, fb, tab, inverse, hi, lo, tiles, sems)


def product_kernel(hi0, lo0, hi1, lo1, own, other, out, whole):
    core = lax.axis_index("core")
    for k in range(4):
        for y in range(4):
            base = 256 * (k % 2) + 64 * y
            at = pl.multiple_of(base + 32 * core, 32)
            whole[k // 2, pl.ds(at, 32), :] = own[y, k]
            at = pl.multiple_of(base + 32 * (1 - core), 32)
            whole[k // 2, pl.ds(at, 32), :] = other[y, k]
    for f in range(2):
        w = split(whole[f])
        hi, lo = ((hi0, lo0), (hi1, lo1))[f]
        for s in range(4):
            total = dot3((hi[s], lo[s]), w, ((1,), (0,)))
            for x in range(4):
                for z in range(4):
                    at = 64 * x + 16 * z
                    first = jnp.where(core == 0, x, z)
                    second = jnp.where(core == 0, z, x)
                    out[first, second, 4 * f + s] = total[at : at + 16, :]


def half_kernel(inc, out):
    for d in range(4):
        for k in range(8):
            out[d, k] = (inc[0, d, k] + inc[1, d, k]) + (inc[2, d, k] + inc[3, d, k])


def reduce_kernel(tab, mask, parts, mine, out):
    for d in range(8):
        out[d, 0:32] = jnp.zeros((32, 256), F32)
    for f in range(2):
        rows = []
        for s in range(4):
            k = 4 * f + s
            v = (parts[0, k] + parts[1, k]) + (parts[2, k] + parts[3, k])
            rows.append(v)
            out[tab[16 * f + s] >> 2, 16 * f : 16 * f + 16] = -v
        left = mine[4 * f : 4 * f + 4].reshape(64, 256)
        right = jnp.concatenate(rows, axis=0)
        full = dot3(split(left), split(right), ((0,), (0,)))
        full = full * mask[f]
        packed = full[:, :128] + full[:, 128:]
        for d in range(4):
            part = packed[64 * d : 64 * d + 64]
            out[4 * f + d, 32:64] = jnp.concatenate([part[:32], part[32:]], axis=1)


def place_kernel(fb, inc, out):
    r = lax.axis_index("y") * 2 + lax.axis_index("core")
    total = inc[0, 32:64]
    for d in range(1, 8):
        total = total + inc[d, 32:64]
    for d in range(4):
        out[d, 32:64] = total
    for f in range(2):
        for i in range(4):
            out[i, 16 * f : 16 * f + 16] = inc[fb[f, 4 * r + i] >> 3, 16 * f : 16 * f + 16, :]


def border_kernel(inc, border):
    for z in range(4):
        for f in range(2):
            border[f, 16 * z : 16 * z + 16] = inc[z, 16 * f : 16 * f + 16, :]


def spread_kernel(inc, out):
    total = (inc[0, 32:64] + inc[1, 32:64]) + (inc[2, 32:64] + inc[3, 32:64])
    for d in range(16):
        out[d] = total


def chunk_kernel(inc, out):
    for y in range(4):
        at = 4 * y
        out[y] = (inc[at] + inc[at + 1]) + (inc[at + 2] + inc[at + 3])


def finish_kernel(own, other, mask, terms, out, chunks):
    core = lax.axis_index("core")
    for y in range(4):
        chunks[2 * y + core] = own[y]
        chunks[2 * y + 1 - core] = other[y]
    for f in range(2):
        for d in range(4):
            v = chunks[4 * f + d]
            v = jnp.concatenate([v[:, :128], v[:, 128:]], axis=0)
            at = slice(64 * d, 64 * d + 64)
            out[f, at] = mask[f, at] * (terms[f, at] + jnp.concatenate([v, v], axis=1))


def call(kernel, ins, out_shape, out_specs=None, scratch=(), limit=8, cost=None):
    if out_specs is None:
        out_specs = jax.tree.map(lambda _: VMEM, out_shape)
    return pl.pallas_call(
        kernel,
        in_specs=ins,
        out_shape=out_shape,
        out_specs=out_specs,
        scratch_shapes=scratch,
        cost_estimate=cost,
        compiler_params=pltpu.CompilerParams(vmem_limit_bytes=limit * MIB),
    )


def a2a(v, axes):
    return lax.all_to_all(v, axes, 0, 0, tiled=True)


def grouped(v, stage):
    groups = []
    for line in range(8):
        for o in range(4):
            along_x = [16 * line + 4 * o + i for i in range(4)]
            along_z = [16 * line + 4 * i + o for i in range(4)]
            groups.append(along_x if line % 2 == stage else along_z)
    return lax.all_to_all(v, ALL, 0, 0, tiled=True, axis_index_groups=groups)


def hbm(v):
    return pltpu.with_memory_space_constraint(v, pltpu.HBM)


def swap(v):
    return lax.ppermute(v, "core", [(0, 1), (1, 0)])


def body(inverse, fb, panels, terms, bounds):
    outgoing = call(
        pack_kernel,
        [SMEM, ANY],
        sds((8, 96, 256)),
        ANY,
        scratch=[
            pltpu.VMEM((8, 96, 256), F32),
            pltpu.SemaphoreType.DMA((18,)),
            pltpu.SemaphoreType.DMA((3,)),
        ],
    )(hbm(fb), hbm(panels.reshape(2, 4, 8, 32, 256)))
    incoming = a2a(outgoing, ROW)
    tiles = (sds((4, 256, 512), BF16), sds((4, 256, 512), BF16))
    buffers = [pltpu.VMEM((8, 256, 256), F32), pltpu.SemaphoreType.DMA((8,))]
    cost = pl.CostEstimate(flops=2 * MIB, bytes_accessed=6 * MIB, transcendentals=0)
    hi0, lo0, tab, mask = call(
        first_kernel,
        [SMEM, SMEM, ANY],
        (*tiles, sds((32,), jnp.int32), sds((2, 256, 256))),
        (VMEM, VMEM, SMEM, VMEM),
        scratch=buffers,
        limit=16,
        cost=cost,
    )(fb, bounds, hbm(inverse))
    slices, mine = call(
        pick_kernel, [SMEM, VMEM], (sds((4, 4, 32, 256)), sds((8, 16, 256)))
    )(tab, incoming)
    own = a2a(slices, "y")
    other = swap(own)
    hi1, lo1 = call(
        second_kernel, [SMEM, SMEM, ANY, ANY], tiles, scratch=buffers, limit=16, cost=cost
    )(fb, tab, hbm(inverse), own)
    parts = call(
        product_kernel,
        [VMEM] * 6,
        sds((4, 4, 8, 16, 256)),
        scratch=[pltpu.VMEM((2, 512, 256), F32)],
        limit=16,
    )(hi0, lo0, hi1, lo1, own, other)
    parts = grouped(parts, 0)
    parts = call(half_kernel, [VMEM], sds((4, 8, 16, 256)))(parts)
    parts = grouped(parts, 1)
    v = call(reduce_kernel, [SMEM, VMEM, VMEM, VMEM], sds((8, 64, 256)))(tab, mask, parts, mine)
    v = a2a(v, ROW)
    v = call(place_kernel, [SMEM, VMEM], sds((4, 64, 256)))(fb, v)
    v = a2a(v, "z")
    sums = call(spread_kernel, [VMEM], sds((16, 32, 256)))(v)
    sums = a2a(sums, ("y", "x"))
    own = call(chunk_kernel, [VMEM], sds((4, 32, 256)))(sums)
    other = swap(own)
    v, own = lax.optimization_barrier((v, own))
    border = call(border_kernel, [VMEM], sds((2, 64, 256)))(v)
    diag = call(
        finish_kernel,
        [VMEM, VMEM, VMEM, VMEM],
        sds((2, 256, 256)),
        scratch=[pltpu.VMEM((8, 32, 256), F32)],
    )(own, other, mask, terms)
    return border, diag


def solution(mesh):
    grid = Mesh(mesh.devices.reshape(4, 2, 4, 4), ALL)
    placed = (P(ROW, COL), P(), P(None, ROW, None), P(), P())
    return jax.shard_map(
        body,
        mesh=grid,
        in_specs=placed,
        out_specs=(P(None, ALL, None), P()),
        check_vma=False,
    )
```

```python
import jax
import jax.numpy as jnp
from jax import lax
from jax.experimental import pallas as pl
from jax.experimental.pallas import tpu as pltpu
from jax.sharding import Mesh, PartitionSpec as P

F32 = jnp.float32
BF16 = jnp.bfloat16
ROW = ("y", "core")
COL = ("z", "x")
ALL = ("y", "core", "z", "x")
VMEM = pl.BlockSpec(memory_space=pltpu.VMEM)
SMEM = pl.BlockSpec(memory_space=pltpu.SMEM)
ANY = pl.BlockSpec(memory_space=pl.ANY)
MIB = 1024 * 1024


def sds(shape, dtype=F32):
    return jax.ShapeDtypeStruct(shape, dtype)


def split(v):
    hi = v.astype(BF16)
    lo = (v - hi.astype(F32)).astype(BF16)
    return hi, lo


def dot3(a, b, dims):
    (ah, al), (bh, bl) = a, b
    mm = lambda p, q: lax.dot_general(p, q, (dims, ((), ())), preferred_element_type=F32)
    return mm(ah, bh) + (mm(ah, bl) + mm(al, bh))


def pack_kernel(fb, w, out, stage, ins, outs):
    r = lax.axis_index("y") * 2 + lax.axis_index("core")
    z, x = lax.axis_index("z"), lax.axis_index("x")
    c = z * 4 + x
    part = 2 * x + z // 2
    row = pl.multiple_of(16 * (z % 2), 16)
    pieces, mine = [], []
    for f in range(2):
        own = [fb[f, 4 * r + i] for i in range(4)]
        piece = jnp.int32(0)
        for i in range(1, 4):
            piece = jnp.where((own[i] >> 2) == c, i, piece)
        at = (slice(None), slice(32 * f, 32 * f + 32))
        copy = pltpu.make_async_copy(w.at[f, piece], stage.at[at], ins.at[f])
        copy.start()
        pieces.append((copy, pltpu.make_async_copy(stage.at[at], out.at[at], outs.at[f])))
    for f in range(2):
        own = [fb[f, 4 * r + i] for i in range(4)]
        for d in range(8):
            named = jnp.int32(0)
            for i in range(1, 4):
                named = jnp.where((own[i] >> 3) == d, i, named)
            copy = pltpu.make_async_copy(
                w.at[f, named, part, pl.ds(row, 16)],
                stage.at[d, 64 + 16 * f : 80 + 16 * f],
                ins.at[2 + 8 * f + d],
            )
            copy.start()
            mine.append(copy)
    for first, second in pieces:
        first.wait()
        second.start()
    for copy in mine:
        copy.wait()
    at = (slice(None), slice(64, 96))
    last = pltpu.make_async_copy(stage.at[at], out.at[at], outs.at[2])
    last.start()
    for first, second in pieces:
        second.wait()
    last.wait()


def pick_kernel(tab, inc, slices, mine):
    for f in range(2):
        for t in range(2):
            p = tab[16 * f + 8 + t]
            slices[2 * f + t] = inc[p >> 2, 32 * f : 32 * f + 32, :]
        for s in range(4):
            p = tab[16 * f + s]
            mine[4 * f + s] = inc[p >> 2, 64 + 16 * f : 80 + 16 * f, :]


def same_node(bounds, f):
    a = lax.broadcasted_iota(jnp.int32, (256, 256), 0)
    b = lax.broadcasted_iota(jnp.int32, (256, 256), 1)
    ia = jnp.zeros((256, 256), jnp.int32)
    ib = jnp.zeros((256, 256), jnp.int32)
    end = jnp.int32(0)
    for k in range(4):
        end = end + bounds[f, k]
        ia = ia + (a >= end).astype(jnp.int32)
        ib = ib + (b >= end).astype(jnp.int32)
    return ia == ib


def fetch_tiles(f, fb, tab, inverse, hi, lo, tiles, sems):
    copies = []
    for s in range(4):
        for t in range(2):
            k = 2 * s + t
            rb = fb[f, tab[16 * f + s]] & 7
            cb = fb[f, tab[16 * f + 8 + t]] & 3
            src = inverse.at[
                pl.ds(pl.multiple_of(rb * 256, 256), 256),
                pl.ds(pl.multiple_of(cb * 256, 256), 256),
            ]
            copy = pltpu.make_async_copy(src, tiles.at[k], sems.at[k])
            copy.start()
            copies.append(copy)
    for k in range(8):
        copies[k].wait()
        h, l = split(tiles[k])
        hi[k // 2, :, 256 * (k % 2) : 256 * (k % 2) + 256] = h
        lo[k // 2, :, 256 * (k % 2) : 256 * (k % 2) + 256] = l


def first_kernel(fb, bounds, inverse, hi, lo, tab, mask, tiles, sems):
    r = lax.axis_index("y") * 2 + lax.axis_index("core")
    c = lax.axis_index("z") * 4 + lax.axis_index("x")
    for k in range(32):
        tab[k] = 0
    for f in range(2):
        rows = jnp.int32(0)
        cols = jnp.int32(0)
        for p in range(32):
            b = fb[f, p]
            tab[16 * f + rows] = p
            rows = rows + ((b >> 3) == r).astype(jnp.int32)
            tab[16 * f + 8 + cols] = p
            cols = cols + ((b >> 2) == c).astype(jnp.int32)
    for f in range(2):
        mask[f] = same_node(bounds, f).astype(F32)
    fetch_tiles(0, fb, tab, inverse, hi, lo, tiles, sems)


def second_kernel(fb, tab, inverse, after, hi, lo, tiles, sems):
    fetch_tiles(1, fb, tab, inverse, hi, lo, tiles, sems)


def product_kernel(hi0, lo0, hi1, lo1, *refs):
    own, other, (out, whole) = refs[:4], refs[4:8], refs[8:]
    here = lax.axis_index("y")
    core = lax.axis_index("core")
    for step, mine, theirs in zip((0, 1, 3, 2), own, other):
        y = (here - step) & 3
        for k in range(4):
            base = 256 * (k % 2) + 64 * y
            at = pl.multiple_of(base + 32 * core, 32)
            whole[k // 2, pl.ds(at, 32), :] = mine[k]
            at = pl.multiple_of(base + 32 * (1 - core), 32)
            whole[k // 2, pl.ds(at, 32), :] = theirs[k]
    for f in range(2):
        w = split(whole[f])
        hi, lo = ((hi0, lo0), (hi1, lo1))[f]
        for s in range(4):
            total = dot3((hi[s], lo[s]), w, ((1,), (0,)))
            for x in range(4):
                for z in range(4):
                    at = 64 * x + 16 * z
                    first = jnp.where(core == 0, x, z)
                    second = jnp.where(core == 0, z, x)
                    out[first, second, 4 * f + s] = total[at : at + 16, :]


def half_kernel(inc, out):
    for d in range(4):
        for k in range(8):
            out[d, k] = (inc[0, d, k] + inc[1, d, k]) + (inc[2, d, k] + inc[3, d, k])


def reduce_kernel(tab, mask, parts, mine, *refs):
    outs, buf = refs[:4], refs[4]
    core, here = lax.axis_index("core"), lax.axis_index("y")
    for step in range(4):
        for rel in range(2):
            buf[step, rel, 0:32] = jnp.zeros((32, 256), F32)
    for f in range(2):
        rows = []
        for s in range(4):
            k = 4 * f + s
            v = (parts[0, k] + parts[1, k]) + (parts[2, k] + parts[3, k])
            rows.append(v)
            owner = tab[16 * f + s] >> 2
            step, rel = ((owner >> 1) - here) & 3, (owner & 1) ^ core
            buf[step, rel, 16 * f : 16 * f + 16] = -v
        left = mine[4 * f : 4 * f + 4].reshape(64, 256)
        right = jnp.concatenate(rows, axis=0)
        full = dot3(split(left), split(right), ((0,), (0,)))
        full = full * mask[f]
        packed = full[:, :128] + full[:, 128:]
        for d in range(4):
            part = packed[64 * d : 64 * d + 64]
            owner = 4 * f + d
            step, rel = (owner // 2 - here) & 3, (owner % 2) ^ core
            buf[step, rel, 32:64] = jnp.concatenate([part[:32], part[32:]], axis=1)
    for step in range(4):
        outs[step][...] = buf[step]


def place_kernel(fb, *refs):
    own, other, outs, got = refs[:4], refs[4:8], refs[8:12], refs[12]
    core, here = lax.axis_index("core"), lax.axis_index("y")
    z = lax.axis_index("z")
    total = None
    for step in range(4):
        y = (here - step) & 3
        got[0, y] = own[step][0, 0:32]
        got[1, y] = other[step][1, 0:32]
        both = own[step][0, 32:64] + other[step][1, 32:64]
        total = both if total is None else total + both
    for step in range(4):
        i = (z + step) & 3
        for f in range(2):
            source = fb[f, 4 * (2 * here + core) + i] >> 3
            v = got[(source & 1) ^ core, source >> 1, 16 * f : 16 * f + 16, :]
            outs[step][16 * f : 16 * f + 16] = v
        outs[step][32:64] = total


def border_kernel(*refs):
    border = refs[4]
    z = lax.axis_index("z")
    for step in range(4):
        at = pl.multiple_of(16 * ((z - step) & 3), 16)
        for f in range(2):
            border[f, pl.ds(at, 16), :] = refs[step][16 * f : 16 * f + 16]


def spread_kernel(*refs):
    out, got = refs[4:]
    z = lax.axis_index("z")
    for step in range(4):
        got[(z - step) & 3] = refs[step][32:64]
    total = (got[0] + got[1]) + (got[2] + got[3])
    for d in range(16):
        out[d] = total


def chunk_kernel(inc, out):
    for y in range(4):
        at = 4 * y
        out[y] = (inc[at] + inc[at + 1]) + (inc[at + 2] + inc[at + 3])


def finish_kernel(own, other, mask, terms, out, chunks):
    core = lax.axis_index("core")
    for y in range(4):
        chunks[2 * y + core] = own[y]
        chunks[2 * y + 1 - core] = other[y]
    for f in range(2):
        for d in range(4):
            v = chunks[4 * f + d]
            v = jnp.concatenate([v[:, :128], v[:, 128:]], axis=0)
            at = slice(64 * d, 64 * d + 64)
            out[f, at] = mask[f, at] * (terms[f, at] + jnp.concatenate([v, v], axis=1))


def call(kernel, ins, out_shape, out_specs=None, scratch=(), limit=8, cost=None):
    if out_specs is None:
        out_specs = jax.tree.map(lambda _: VMEM, out_shape)
    return pl.pallas_call(
        kernel,
        in_specs=ins,
        out_shape=out_shape,
        out_specs=out_specs,
        scratch_shapes=scratch,
        cost_estimate=cost,
        compiler_params=pltpu.CompilerParams(vmem_limit_bytes=limit * MIB),
    )


def a2a(v, axes):
    return lax.all_to_all(v, axes, 0, 0, tiled=True)


def grouped(v, stage):
    groups = []
    for line in range(8):
        for o in range(4):
            along_x = [16 * line + 4 * o + i for i in range(4)]
            along_z = [16 * line + 4 * i + o for i in range(4)]
            groups.append(along_x if line % 2 == stage else along_z)
    return lax.all_to_all(v, ALL, 0, 0, tiled=True, axis_index_groups=groups)


def hbm(v):
    return pltpu.with_memory_space_constraint(v, pltpu.HBM)


def shift(v, axis, step):
    return lax.ppermute(v, axis, [(i, (i + step) % 4) for i in range(4)])


def swap(v):
    return lax.ppermute(v, "core", [(0, 1), (1, 0)])


def body(inverse, fb, panels, terms, bounds):
    outgoing = call(
        pack_kernel,
        [SMEM, ANY],
        sds((8, 96, 256)),
        ANY,
        scratch=[
            pltpu.VMEM((8, 96, 256), F32),
            pltpu.SemaphoreType.DMA((18,)),
            pltpu.SemaphoreType.DMA((3,)),
        ],
    )(hbm(fb), hbm(panels.reshape(2, 4, 8, 32, 256)))
    incoming = a2a(outgoing, ROW)
    tiles = (sds((4, 256, 512), BF16), sds((4, 256, 512), BF16))
    buffers = [pltpu.VMEM((8, 256, 256), F32), pltpu.SemaphoreType.DMA((8,))]
    cost = pl.CostEstimate(flops=2 * MIB, bytes_accessed=6 * MIB, transcendentals=0)
    hi0, lo0, tab, mask = call(
        first_kernel,
        [SMEM, SMEM, ANY],
        (*tiles, sds((32,), jnp.int32), sds((2, 256, 256))),
        (VMEM, VMEM, SMEM, VMEM),
        scratch=buffers,
        limit=16,
        cost=cost,
    )(fb, bounds, hbm(inverse))
    slices, mine = call(
        pick_kernel, [SMEM, VMEM], (sds((4, 32, 256)), sds((8, 16, 256)))
    )(tab, incoming)
    own = [slices]
    for step in (1, 3, 2):
        own.append(shift(slices, "y", step))
    hi1, lo1 = call(
        second_kernel, [SMEM, SMEM, ANY, ANY], tiles, scratch=buffers, limit=16, cost=cost
    )(fb, tab, hbm(inverse), slices)
    own[2], hi1 = lax.optimization_barrier((own[2], hi1))
    own[3], hi1 = lax.optimization_barrier((own[3], hi1))
    other = [swap(v) for v in own]
    parts = call(
        product_kernel,
        [VMEM] * 12,
        sds((4, 4, 8, 16, 256)),
        scratch=[pltpu.VMEM((2, 512, 256), F32)],
        limit=16,
    )(hi0, lo0, hi1, lo1, *own, *other)
    parts = grouped(parts, 0)
    parts = call(half_kernel, [VMEM], sds((4, 8, 16, 256)))(parts)
    parts = grouped(parts, 1)
    pair = sds((2, 64, 256))
    outs = call(
        reduce_kernel,
        [SMEM, VMEM, VMEM, VMEM],
        (pair,) * 4,
        scratch=[pltpu.VMEM((4, 2, 64, 256), F32)],
    )(tab, mask, parts, mine)
    own = [outs[0]] + [None] * 3
    for step in (1, 3, 2):
        own[step] = shift(outs[step], "y", step)
    other = [swap(v) for v in own]
    outs = call(
        place_kernel,
        [SMEM] + [VMEM] * 8,
        (sds((64, 256)),) * 4,
        scratch=[pltpu.VMEM((2, 4, 32, 256), F32)],
    )(fb, *own, *other)
    v = [outs[0]] + [None] * 3
    for step in (1, 3, 2):
        v[step] = shift(outs[step], "z", step)
    sums = call(
        spread_kernel,
        [VMEM] * 4,
        sds((16, 32, 256)),
        scratch=[pltpu.VMEM((4, 32, 256), F32)],
    )(*v)
    sums = a2a(sums, ("y", "x"))
    own = call(chunk_kernel, [VMEM], sds((4, 32, 256)))(sums)
    other = swap(own)
    v, own = lax.optimization_barrier((v, own))
    border = call(border_kernel, [VMEM] * 4, sds((2, 64, 256)))(*v)
    diag = call(
        finish_kernel,
        [VMEM, VMEM, VMEM, VMEM],
        sds((2, 256, 256)),
        scratch=[pltpu.VMEM((8, 32, 256), F32)],
    )(own, other, mask, terms)
    return border, diag


def solution(mesh):
    grid = Mesh(mesh.devices.reshape(4, 2, 4, 4), ALL)
    placed = (P(ROW, COL), P(), P(None, ROW, None), P(), P())
    return jax.shard_map(
        body,
        mesh=grid,
        in_specs=placed,
        out_specs=(P(None, ALL, None), P()),
        check_vma=False,
    )
```

```python
import jax
import jax.numpy as jnp
from jax import lax
from jax.experimental import pallas as pl
from jax.experimental.pallas import tpu as pltpu
from jax.sharding import Mesh, PartitionSpec as P

F32 = jnp.float32
BF16 = jnp.bfloat16
ROW = ("y", "core")
COL = ("z", "x")
ALL = ("y", "core", "z", "x")
VMEM = pl.BlockSpec(memory_space=pltpu.VMEM)
SMEM = pl.BlockSpec(memory_space=pltpu.SMEM)
ANY = pl.BlockSpec(memory_space=pl.ANY)
MIB = 1024 * 1024


def sds(shape, dtype=F32):
    return jax.ShapeDtypeStruct(shape, dtype)


def split(v):
    hi = v.astype(BF16)
    lo = (v - hi.astype(F32)).astype(BF16)
    return hi, lo


def dot3(a, b, dims):
    (ah, al), (bh, bl) = a, b
    mm = lambda p, q: lax.dot_general(p, q, (dims, ((), ())), preferred_element_type=F32)
    return mm(ah, bh) + (mm(ah, bl) + mm(al, bh))


def pack_kernel(fb, w, out, stage, ins, outs):
    r = lax.axis_index("y") * 2 + lax.axis_index("core")
    z, x = lax.axis_index("z"), lax.axis_index("x")
    c = z * 4 + x
    part = 2 * x + z // 2
    row = pl.multiple_of(16 * (z % 2), 16)
    pieces, mine = [], []
    for f in range(2):
        own = [fb[f, 4 * r + i] for i in range(4)]
        piece = jnp.int32(0)
        for i in range(1, 4):
            piece = jnp.where((own[i] >> 2) == c, i, piece)
        at = (slice(None), slice(32 * f, 32 * f + 32))
        copy = pltpu.make_async_copy(w.at[f, piece], stage.at[at], ins.at[f])
        copy.start()
        pieces.append((copy, pltpu.make_async_copy(stage.at[at], out.at[at], outs.at[f])))
    for f in range(2):
        own = [fb[f, 4 * r + i] for i in range(4)]
        for d in range(8):
            named = jnp.int32(0)
            for i in range(1, 4):
                named = jnp.where((own[i] >> 3) == d, i, named)
            copy = pltpu.make_async_copy(
                w.at[f, named, part, pl.ds(row, 16)],
                stage.at[d, 64 + 16 * f : 80 + 16 * f],
                ins.at[2 + 8 * f + d],
            )
            copy.start()
            mine.append(copy)
    for first, second in pieces:
        first.wait()
        second.start()
    for copy in mine:
        copy.wait()
    at = (slice(None), slice(64, 96))
    last = pltpu.make_async_copy(stage.at[at], out.at[at], outs.at[2])
    last.start()
    for first, second in pieces:
        second.wait()
    last.wait()


def pick_kernel(tab, inc, slices, mine):
    for f in range(2):
        for t in range(2):
            p = tab[16 * f + 8 + t]
            slices[2 * f + t] = inc[p >> 2, 32 * f : 32 * f + 32, :]
        for s in range(4):
            p = tab[16 * f + s]
            mine[4 * f + s] = inc[p >> 2, 64 + 16 * f : 80 + 16 * f, :]


def same_node(bounds, f):
    a = lax.broadcasted_iota(jnp.int32, (256, 256), 0)
    b = lax.broadcasted_iota(jnp.int32, (256, 256), 1)
    ia = jnp.zeros((256, 256), jnp.int32)
    ib = jnp.zeros((256, 256), jnp.int32)
    end = jnp.int32(0)
    for k in range(4):
        end = end + bounds[f, k]
        ia = ia + (a >= end).astype(jnp.int32)
        ib = ib + (b >= end).astype(jnp.int32)
    return ia == ib


def fetch_tiles(f, fb, tab, inverse, hi, lo, tiles, sems):
    copies = []
    for s in range(4):
        for t in range(2):
            k = 2 * s + t
            rb = fb[f, tab[16 * f + s]] & 7
            cb = fb[f, tab[16 * f + 8 + t]] & 3
            src = inverse.at[
                pl.ds(pl.multiple_of(rb * 256, 256), 256),
                pl.ds(pl.multiple_of(cb * 256, 256), 256),
            ]
            copy = pltpu.make_async_copy(src, tiles.at[k], sems.at[k])
            copy.start()
            copies.append(copy)
    for k in range(8):
        copies[k].wait()
        h, l = split(tiles[k])
        hi[k // 2, :, 256 * (k % 2) : 256 * (k % 2) + 256] = h
        lo[k // 2, :, 256 * (k % 2) : 256 * (k % 2) + 256] = l


def first_kernel(fb, bounds, inverse, hi, lo, tab, mask, tiles, sems):
    r = lax.axis_index("y") * 2 + lax.axis_index("core")
    c = lax.axis_index("z") * 4 + lax.axis_index("x")
    for k in range(32):
        tab[k] = 0
    for f in range(2):
        rows = jnp.int32(0)
        cols = jnp.int32(0)
        for p in range(32):
            b = fb[f, p]
            tab[16 * f + rows] = p
            rows = rows + ((b >> 3) == r).astype(jnp.int32)
            tab[16 * f + 8 + cols] = p
            cols = cols + ((b >> 2) == c).astype(jnp.int32)
    for f in range(2):
        mask[f] = same_node(bounds, f).astype(F32)
    fetch_tiles(0, fb, tab, inverse, hi, lo, tiles, sems)


def second_kernel(fb, tab, inverse, after, hi, lo, tiles, sems):
    fetch_tiles(1, fb, tab, inverse, hi, lo, tiles, sems)


def product_kernel(hi0, lo0, hi1, lo1, *refs):
    own, other, (out, whole) = refs[:4], refs[4:8], refs[8:]
    here = lax.axis_index("y")
    core = lax.axis_index("core")
    for step, mine, theirs in zip((0, 1, 3, 2), own, other):
        y = (here - step) & 3
        for k in range(4):
            base = 256 * (k % 2) + 64 * y
            at = pl.multiple_of(base + 32 * core, 32)
            whole[k // 2, pl.ds(at, 32), :] = mine[k]
            at = pl.multiple_of(base + 32 * (1 - core), 32)
            whole[k // 2, pl.ds(at, 32), :] = theirs[k]
    for f in range(2):
        w = split(whole[f])
        hi, lo = ((hi0, lo0), (hi1, lo1))[f]
        for s in range(4):
            total = dot3((hi[s], lo[s]), w, ((1,), (0,)))
            for x in range(4):
                for z in range(4):
                    at = 64 * x + 16 * z
                    first = jnp.where(core == 0, x, z)
                    second = jnp.where(core == 0, z, x)
                    out[first, second, 4 * f + s] = total[at : at + 16, :]


def half_kernel(inc, *outs):
    core = lax.axis_index("core")
    z, x = lax.axis_index("z"), lax.axis_index("x")
    here = jnp.where(core == 0, z, x)
    for step in range(4):
        d = (here + step) & 3
        for k in range(8):
            outs[step][k] = (inc[0, d, k] + inc[1, d, k]) + (inc[2, d, k] + inc[3, d, k])


def reduce_kernel(tab, mask, mine, *refs):
    parts, outs, buf = refs[:4], refs[4:8], refs[8]
    core, here = lax.axis_index("core"), lax.axis_index("y")
    for step in range(4):
        for rel in range(2):
            buf[step, rel, 0:32] = jnp.zeros((32, 256), F32)
    for f in range(2):
        rows = []
        for s in range(4):
            k = 4 * f + s
            v = (parts[0][k] + parts[1][k]) + (parts[2][k] + parts[3][k])
            rows.append(v)
            owner = tab[16 * f + s] >> 2
            step, rel = ((owner >> 1) - here) & 3, (owner & 1) ^ core
            buf[step, rel, 16 * f : 16 * f + 16] = -v
        left = mine[4 * f : 4 * f + 4].reshape(64, 256)
        right = jnp.concatenate(rows, axis=0)
        full = dot3(split(left), split(right), ((0,), (0,)))
        full = full * mask[f]
        packed = full[:, :128] + full[:, 128:]
        for d in range(4):
            part = packed[64 * d : 64 * d + 64]
            owner = 4 * f + d
            step, rel = (owner // 2 - here) & 3, (owner % 2) ^ core
            buf[step, rel, 32:64] = jnp.concatenate([part[:32], part[32:]], axis=1)
    for step in range(4):
        outs[step][...] = buf[step]


def place_kernel(fb, *refs):
    own, other, outs, got = refs[:4], refs[4:8], refs[8:12], refs[12]
    core, here = lax.axis_index("core"), lax.axis_index("y")
    z = lax.axis_index("z")
    total = None
    for step in range(4):
        y = (here - step) & 3
        got[0, y] = own[step][0, 0:32]
        got[1, y] = other[step][1, 0:32]
        both = own[step][0, 32:64] + other[step][1, 32:64]
        total = both if total is None else total + both
    for step in range(4):
        i = (z + step) & 3
        for f in range(2):
            source = fb[f, 4 * (2 * here + core) + i] >> 3
            v = got[(source & 1) ^ core, source >> 1, 16 * f : 16 * f + 16, :]
            outs[step][16 * f : 16 * f + 16] = v
        outs[step][32:64] = total


def border_kernel(*refs):
    border = refs[4]
    z = lax.axis_index("z")
    for step in range(4):
        at = pl.multiple_of(16 * ((z - step) & 3), 16)
        for f in range(2):
            border[f, pl.ds(at, 16), :] = refs[step][16 * f : 16 * f + 16]


def spread_kernel(*refs):
    out, got = refs[4:]
    z = lax.axis_index("z")
    for step in range(4):
        got[(z - step) & 3] = refs[step][32:64]
    total = (got[0] + got[1]) + (got[2] + got[3])
    for d in range(16):
        out[d] = total


def chunk_kernel(inc, out):
    for y in range(4):
        at = 4 * y
        out[y] = (inc[at] + inc[at + 1]) + (inc[at + 2] + inc[at + 3])


def finish_kernel(own, other, mask, terms, out, chunks):
    core = lax.axis_index("core")
    for y in range(4):
        chunks[2 * y + core] = own[y]
        chunks[2 * y + 1 - core] = other[y]
    for f in range(2):
        for d in range(4):
            v = chunks[4 * f + d]
            v = jnp.concatenate([v[:, :128], v[:, 128:]], axis=0)
            at = slice(64 * d, 64 * d + 64)
            out[f, at] = mask[f, at] * (terms[f, at] + jnp.concatenate([v, v], axis=1))


def call(kernel, ins, out_shape, out_specs=None, scratch=(), limit=8, cost=None):
    if out_specs is None:
        out_specs = jax.tree.map(lambda _: VMEM, out_shape)
    return pl.pallas_call(
        kernel,
        in_specs=ins,
        out_shape=out_shape,
        out_specs=out_specs,
        scratch_shapes=scratch,
        cost_estimate=cost,
        compiler_params=pltpu.CompilerParams(vmem_limit_bytes=limit * MIB),
    )


def a2a(v, axes):
    return lax.all_to_all(v, axes, 0, 0, tiled=True)


def grouped(v):
    groups = []
    for line in range(8):
        for o in range(4):
            along_x = [16 * line + 4 * o + i for i in range(4)]
            along_z = [16 * line + 4 * i + o for i in range(4)]
            groups.append(along_z if line % 2 else along_x)
    return lax.all_to_all(v, ALL, 0, 0, tiled=True, axis_index_groups=groups)


def step_groups(v, step):
    pairs = []
    for line in range(8):
        for z in range(4):
            for x in range(4):
                to = (4 * z + (x + step) % 4) if line % 2 else (4 * ((z + step) % 4) + x)
                pairs.append((16 * line + 4 * z + x, 16 * line + to))
    return lax.ppermute(v, ALL, pairs)


def hbm(v):
    return pltpu.with_memory_space_constraint(v, pltpu.HBM)


def shift(v, axis, step):
    return lax.ppermute(v, axis, [(i, (i + step) % 4) for i in range(4)])


def swap(v):
    return lax.ppermute(v, "core", [(0, 1), (1, 0)])


def body(inverse, fb, panels, terms, bounds):
    outgoing = call(
        pack_kernel,
        [SMEM, ANY],
        sds((8, 96, 256)),
        ANY,
        scratch=[
            pltpu.VMEM((8, 96, 256), F32),
            pltpu.SemaphoreType.DMA((18,)),
            pltpu.SemaphoreType.DMA((3,)),
        ],
    )(hbm(fb), hbm(panels.reshape(2, 4, 8, 32, 256)))
    incoming = a2a(outgoing, ROW)
    tiles = (sds((4, 256, 512), BF16), sds((4, 256, 512), BF16))
    buffers = [pltpu.VMEM((8, 256, 256), F32), pltpu.SemaphoreType.DMA((8,))]
    cost = pl.CostEstimate(flops=2 * MIB, bytes_accessed=6 * MIB, transcendentals=0)
    hi0, lo0, tab, mask = call(
        first_kernel,
        [SMEM, SMEM, ANY],
        (*tiles, sds((32,), jnp.int32), sds((2, 256, 256))),
        (VMEM, VMEM, SMEM, VMEM),
        scratch=buffers,
        limit=16,
        cost=cost,
    )(fb, bounds, hbm(inverse))
    slices, mine = call(
        pick_kernel, [SMEM, VMEM], (sds((4, 32, 256)), sds((8, 16, 256)))
    )(tab, incoming)
    own = [slices]
    for step in (1, 3, 2):
        own.append(shift(slices, "y", step))
    hi1, lo1 = call(
        second_kernel, [SMEM, SMEM, ANY, ANY], tiles, scratch=buffers, limit=16, cost=cost
    )(fb, tab, hbm(inverse), slices)
    own[2], hi1 = lax.optimization_barrier((own[2], hi1))
    own[3], hi1 = lax.optimization_barrier((own[3], hi1))
    other = [swap(v) for v in own]
    parts = call(
        product_kernel,
        [VMEM] * 12,
        sds((4, 4, 8, 16, 256)),
        scratch=[pltpu.VMEM((2, 512, 256), F32)],
        limit=16,
    )(hi0, lo0, hi1, lo1, *own, *other)
    parts = grouped(parts)
    outs = call(half_kernel, [VMEM], (sds((8, 16, 256)),) * 4)(parts)
    parts = [outs[0]] + [None] * 3
    for step in (1, 3, 2):
        parts[step] = step_groups(outs[step], step)
    pair = sds((2, 64, 256))
    outs = call(
        reduce_kernel,
        [SMEM] + [VMEM] * 6,
        (pair,) * 4,
        scratch=[pltpu.VMEM((4, 2, 64, 256), F32)],
    )(tab, mask, mine, *parts)
    own = [outs[0]] + [None] * 3
    for step in (1, 3, 2):
        own[step] = shift(outs[step], "y", step)
    other = [swap(v) for v in own]
    outs = call(
        place_kernel,
        [SMEM] + [VMEM] * 8,
        (sds((64, 256)),) * 4,
        scratch=[pltpu.VMEM((2, 4, 32, 256), F32)],
    )(fb, *own, *other)
    v = [outs[0]] + [None] * 3
    for step in (1, 3, 2):
        v[step] = shift(outs[step], "z", step)
    sums = call(
        spread_kernel,
        [VMEM] * 4,
        sds((16, 32, 256)),
        scratch=[pltpu.VMEM((4, 32, 256), F32)],
    )(*v)
    sums = a2a(sums, ("y", "x"))
    own = call(chunk_kernel, [VMEM], sds((4, 32, 256)))(sums)
    other = swap(own)
    v, own = lax.optimization_barrier((v, own))
    border = call(border_kernel, [VMEM] * 4, sds((2, 64, 256)))(*v)
    diag = call(
        finish_kernel,
        [VMEM, VMEM, VMEM, VMEM],
        sds((2, 256, 256)),
        scratch=[pltpu.VMEM((8, 32, 256), F32)],
    )(own, other, mask, terms)
    return border, diag


def solution(mesh):
    grid = Mesh(mesh.devices.reshape(4, 2, 4, 4), ALL)
    placed = (P(ROW, COL), P(), P(None, ROW, None), P(), P())
    return jax.shard_map(
        body,
        mesh=grid,
        in_specs=placed,
        out_specs=(P(None, ALL, None), P()),
        check_vma=False,
    )
```

```python
import jax
import jax.numpy as jnp
from jax import lax
from jax.experimental import pallas as pl
from jax.experimental.pallas import tpu as pltpu
from jax.sharding import Mesh, PartitionSpec as P

F32 = jnp.float32
BF16 = jnp.bfloat16
ROW = ("y", "core")
COL = ("z", "x")
ALL = ("y", "core", "z", "x")
VMEM = pl.BlockSpec(memory_space=pltpu.VMEM)
SMEM = pl.BlockSpec(memory_space=pltpu.SMEM)
ANY = pl.BlockSpec(memory_space=pl.ANY)
MIB = 1024 * 1024


def sds(shape, dtype=F32):
    return jax.ShapeDtypeStruct(shape, dtype)


def split(v):
    hi = v.astype(BF16)
    lo = (v - hi.astype(F32)).astype(BF16)
    return hi, lo


def dot3(a, b, dims):
    (ah, al), (bh, bl) = a, b
    mm = lambda p, q: lax.dot_general(p, q, (dims, ((), ())), preferred_element_type=F32)
    return mm(ah, bh) + (mm(ah, bl) + mm(al, bh))


def pack_kernel(fb, w, out, stage, ins, outs):
    r = lax.axis_index("y") * 2 + lax.axis_index("core")
    z, x = lax.axis_index("z"), lax.axis_index("x")
    c = z * 4 + x
    part = 2 * x + z // 2
    row = pl.multiple_of(16 * (z % 2), 16)
    pieces, mine = [], []
    for f in range(2):
        own = [fb[f, 4 * r + i] for i in range(4)]
        piece = jnp.int32(0)
        for i in range(1, 4):
            piece = jnp.where((own[i] >> 2) == c, i, piece)
        at = (slice(None), slice(32 * f, 32 * f + 32))
        copy = pltpu.make_async_copy(w.at[f, piece], stage.at[at], ins.at[f])
        copy.start()
        pieces.append((copy, pltpu.make_async_copy(stage.at[at], out.at[at], outs.at[f])))
    for f in range(2):
        own = [fb[f, 4 * r + i] for i in range(4)]
        for d in range(8):
            named = jnp.int32(0)
            for i in range(1, 4):
                named = jnp.where((own[i] >> 3) == d, i, named)
            copy = pltpu.make_async_copy(
                w.at[f, named, part, pl.ds(row, 16)],
                stage.at[d, 64 + 16 * f : 80 + 16 * f],
                ins.at[2 + 8 * f + d],
            )
            copy.start()
            mine.append(copy)
    for first, second in pieces:
        first.wait()
        second.start()
    for copy in mine:
        copy.wait()
    at = (slice(None), slice(64, 96))
    last = pltpu.make_async_copy(stage.at[at], out.at[at], outs.at[2])
    last.start()
    for first, second in pieces:
        second.wait()
    last.wait()


def pick_kernel(tab, inc, slices, mine):
    for f in range(2):
        for t in range(2):
            p = tab[16 * f + 8 + t]
            slices[2 * f + t] = inc[p >> 2, 32 * f : 32 * f + 32, :]
        for s in range(4):
            p = tab[16 * f + s]
            mine[4 * f + s] = inc[p >> 2, 64 + 16 * f : 80 + 16 * f, :]


def same_node(bounds, f):
    a = lax.broadcasted_iota(jnp.int32, (256, 256), 0)
    b = lax.broadcasted_iota(jnp.int32, (256, 256), 1)
    ia = jnp.zeros((256, 256), jnp.int32)
    ib = jnp.zeros((256, 256), jnp.int32)
    end = jnp.int32(0)
    for k in range(4):
        end = end + bounds[f, k]
        ia = ia + (a >= end).astype(jnp.int32)
        ib = ib + (b >= end).astype(jnp.int32)
    return ia == ib


def fetch_tiles(f, fb, tab, inverse, hi, lo, tiles, sems):
    copies = []
    for s in range(4):
        for t in range(2):
            k = 2 * s + t
            rb = fb[f, tab[16 * f + s]] & 7
            cb = fb[f, tab[16 * f + 8 + t]] & 3
            src = inverse.at[
                pl.ds(pl.multiple_of(rb * 256, 256), 256),
                pl.ds(pl.multiple_of(cb * 256, 256), 256),
            ]
            copy = pltpu.make_async_copy(src, tiles.at[k], sems.at[k])
            copy.start()
            copies.append(copy)
    for k in range(8):
        copies[k].wait()
        h, l = split(tiles[k])
        hi[k // 2, :, 256 * (k % 2) : 256 * (k % 2) + 256] = h
        lo[k // 2, :, 256 * (k % 2) : 256 * (k % 2) + 256] = l


def first_kernel(fb, bounds, inverse, hi, lo, tab, mask, tiles, sems):
    r = lax.axis_index("y") * 2 + lax.axis_index("core")
    c = lax.axis_index("z") * 4 + lax.axis_index("x")
    for k in range(32):
        tab[k] = 0
    for f in range(2):
        rows = jnp.int32(0)
        cols = jnp.int32(0)
        for p in range(32):
            b = fb[f, p]
            tab[16 * f + rows] = p
            rows = rows + ((b >> 3) == r).astype(jnp.int32)
            tab[16 * f + 8 + cols] = p
            cols = cols + ((b >> 2) == c).astype(jnp.int32)
    for f in range(2):
        mask[f] = same_node(bounds, f).astype(F32)
    fetch_tiles(0, fb, tab, inverse, hi, lo, tiles, sems)


def second_kernel(fb, tab, inverse, after, hi, lo, tiles, sems):
    fetch_tiles(1, fb, tab, inverse, hi, lo, tiles, sems)


def product_kernel(hi0, lo0, hi1, lo1, *refs):
    own, other, (out, whole) = refs[:4], refs[4:8], refs[8:]
    here = lax.axis_index("y")
    core = lax.axis_index("core")
    for step, mine, theirs in zip((0, 2, 1, 3), own, other):
        y = (here - step) & 3
        for k in range(4):
            base = 256 * (k % 2) + 64 * y
            at = pl.multiple_of(base + 32 * core, 32)
            whole[k // 2, pl.ds(at, 32), :] = mine[k]
            at = pl.multiple_of(base + 32 * (1 - core), 32)
            whole[k // 2, pl.ds(at, 32), :] = theirs[k]
    for f in range(2):
        w = split(whole[f])
        hi, lo = ((hi0, lo0), (hi1, lo1))[f]
        for s in range(4):
            total = dot3((hi[s], lo[s]), w, ((1,), (0,)))
            for x in range(4):
                for z in range(4):
                    at = 64 * x + 16 * z
                    first = jnp.where(core == 0, x, z)
                    second = jnp.where(core == 0, z, x)
                    out[first, second, 4 * f + s] = total[at : at + 16, :]


def half_kernel(inc, *outs):
    core = lax.axis_index("core")
    z, x = lax.axis_index("z"), lax.axis_index("x")
    here = jnp.where(core == 0, z, x)
    for step in range(4):
        d = (here + step) & 3
        for k in range(8):
            outs[step][k] = (inc[0, d, k] + inc[1, d, k]) + (inc[2, d, k] + inc[3, d, k])


def reduce_kernel(tab, mask, mine, *refs):
    parts, outs, buf = refs[:4], refs[4:8], refs[8]
    core, here = lax.axis_index("core"), lax.axis_index("y")
    for step in range(4):
        for rel in range(2):
            buf[step, rel, 0:32] = jnp.zeros((32, 256), F32)
    for f in range(2):
        rows = []
        for s in range(4):
            k = 4 * f + s
            v = (parts[0][k] + parts[1][k]) + (parts[2][k] + parts[3][k])
            rows.append(v)
            owner = tab[16 * f + s] >> 2
            step, rel = ((owner >> 1) - here) & 3, (owner & 1) ^ core
            buf[step, rel, 16 * f : 16 * f + 16] = -v
        left = mine[4 * f : 4 * f + 4].reshape(64, 256)
        right = jnp.concatenate(rows, axis=0)
        full = dot3(split(left), split(right), ((0,), (0,)))
        full = full * mask[f]
        packed = full[:, :128] + full[:, 128:]
        for d in range(4):
            part = packed[64 * d : 64 * d + 64]
            owner = 4 * f + d
            step, rel = (owner // 2 - here) & 3, (owner % 2) ^ core
            buf[step, rel, 32:64] = jnp.concatenate([part[:32], part[32:]], axis=1)
    for step in range(4):
        outs[step][...] = buf[step]


def place_kernel(fb, *refs):
    own, other, outs, got = refs[:4], refs[4:8], refs[8:12], refs[12]
    core, here = lax.axis_index("core"), lax.axis_index("y")
    z = lax.axis_index("z")
    total = None
    for step in range(4):
        y = (here - step) & 3
        got[0, y] = own[step][0, 0:32]
        got[1, y] = other[step][1, 0:32]
        both = own[step][0, 32:64] + other[step][1, 32:64]
        total = both if total is None else total + both
    for step in range(4):
        i = (z + step) & 3
        for f in range(2):
            source = fb[f, 4 * (2 * here + core) + i] >> 3
            v = got[(source & 1) ^ core, source >> 1, 16 * f : 16 * f + 16, :]
            outs[step][16 * f : 16 * f + 16] = v
        outs[step][32:64] = total


def border_kernel(*refs):
    border = refs[4]
    z = lax.axis_index("z")
    for step in range(4):
        at = pl.multiple_of(16 * ((z - step) & 3), 16)
        for f in range(2):
            border[f, pl.ds(at, 16), :] = refs[step][16 * f : 16 * f + 16]


def spread_kernel(*refs):
    out, got = refs[4:]
    z = lax.axis_index("z")
    for step in range(4):
        got[(z - step) & 3] = refs[step][32:64]
    total = (got[0] + got[1]) + (got[2] + got[3])
    for d in range(16):
        out[d] = total


def chunk_kernel(inc, out):
    for y in range(4):
        at = 4 * y
        out[y] = (inc[at] + inc[at + 1]) + (inc[at + 2] + inc[at + 3])


def finish_kernel(own, other, mask, terms, out, chunks):
    core = lax.axis_index("core")
    for y in range(4):
        chunks[2 * y + core] = own[y]
        chunks[2 * y + 1 - core] = other[y]
    for f in range(2):
        for d in range(4):
            v = chunks[4 * f + d]
            v = jnp.concatenate([v[:, :128], v[:, 128:]], axis=0)
            at = slice(64 * d, 64 * d + 64)
            out[f, at] = mask[f, at] * (terms[f, at] + jnp.concatenate([v, v], axis=1))


def call(kernel, ins, out_shape, out_specs=None, scratch=(), limit=8, cost=None):
    if out_specs is None:
        out_specs = jax.tree.map(lambda _: VMEM, out_shape)
    return pl.pallas_call(
        kernel,
        in_specs=ins,
        out_shape=out_shape,
        out_specs=out_specs,
        scratch_shapes=scratch,
        cost_estimate=cost,
        compiler_params=pltpu.CompilerParams(vmem_limit_bytes=limit * MIB),
    )


def a2a(v, axes):
    return lax.all_to_all(v, axes, 0, 0, tiled=True)


def grouped(v):
    groups = []
    for line in range(8):
        for o in range(4):
            along_x = [16 * line + 4 * o + i for i in range(4)]
            along_z = [16 * line + 4 * i + o for i in range(4)]
            groups.append(along_z if line % 2 else along_x)
    return lax.all_to_all(v, ALL, 0, 0, tiled=True, axis_index_groups=groups)


def step_groups(v, step):
    pairs = []
    for line in range(8):
        for z in range(4):
            for x in range(4):
                to = (4 * z + (x + step) % 4) if line % 2 else (4 * ((z + step) % 4) + x)
                pairs.append((16 * line + 4 * z + x, 16 * line + to))
    return lax.ppermute(v, ALL, pairs)


def hbm(v):
    return pltpu.with_memory_space_constraint(v, pltpu.HBM)


def shift(v, axis, step):
    return lax.ppermute(v, axis, [(i, (i + step) % 4) for i in range(4)])


def swap(v):
    return lax.ppermute(v, "core", [(0, 1), (1, 0)])


def body(inverse, fb, panels, terms, bounds):
    outgoing = call(
        pack_kernel,
        [SMEM, ANY],
        sds((8, 96, 256)),
        ANY,
        scratch=[
            pltpu.VMEM((8, 96, 256), F32),
            pltpu.SemaphoreType.DMA((18,)),
            pltpu.SemaphoreType.DMA((3,)),
        ],
    )(hbm(fb), hbm(panels.reshape(2, 4, 8, 32, 256)))
    incoming = a2a(outgoing, ROW)
    tiles = (sds((4, 256, 512), BF16), sds((4, 256, 512), BF16))
    buffers = [pltpu.VMEM((8, 256, 256), F32), pltpu.SemaphoreType.DMA((8,))]
    cost = pl.CostEstimate(flops=2 * MIB, bytes_accessed=6 * MIB, transcendentals=0)
    hi0, lo0, tab, mask = call(
        first_kernel,
        [SMEM, SMEM, ANY],
        (*tiles, sds((32,), jnp.int32), sds((2, 256, 256))),
        (VMEM, VMEM, SMEM, VMEM),
        scratch=buffers,
        limit=16,
        cost=cost,
    )(fb, bounds, hbm(inverse))
    slices, mine = call(
        pick_kernel, [SMEM, VMEM], (sds((4, 32, 256)), sds((8, 16, 256)))
    )(tab, incoming)
    own = [slices]
    for step in (2, 1, 3):
        own.append(shift(slices, "y", step))
    hi1, lo1 = call(
        second_kernel, [SMEM, SMEM, ANY, ANY], tiles, scratch=buffers, limit=16, cost=cost
    )(fb, tab, hbm(inverse), slices)
    own[2], hi1 = lax.optimization_barrier((own[2], hi1))
    own[3], hi1 = lax.optimization_barrier((own[3], hi1))
    other = [swap(v) for v in own]
    parts = call(
        product_kernel,
        [VMEM] * 12,
        sds((4, 4, 8, 16, 256)),
        scratch=[pltpu.VMEM((2, 512, 256), F32)],
        limit=16,
    )(hi0, lo0, hi1, lo1, *own, *other)
    parts = grouped(parts)
    outs = call(half_kernel, [VMEM], (sds((8, 16, 256)),) * 4)(parts)
    parts = [outs[0]] + [None] * 3
    for step in (2, 1, 3):
        parts[step] = step_groups(outs[step], step)
    pair = sds((2, 64, 256))
    outs = call(
        reduce_kernel,
        [SMEM] + [VMEM] * 6,
        (pair,) * 4,
        scratch=[pltpu.VMEM((4, 2, 64, 256), F32)],
    )(tab, mask, mine, *parts)
    own = [outs[0]] + [None] * 3
    for step in (2, 1, 3):
        own[step] = shift(outs[step], "y", step)
    other = [swap(v) for v in own]
    outs = call(
        place_kernel,
        [SMEM] + [VMEM] * 8,
        (sds((64, 256)),) * 4,
        scratch=[pltpu.VMEM((2, 4, 32, 256), F32)],
    )(fb, *own, *other)
    v = [outs[0]] + [None] * 3
    for step in (2, 1, 3):
        v[step] = shift(outs[step], "z", step)
    sums = call(
        spread_kernel,
        [VMEM] * 4,
        sds((16, 32, 256)),
        scratch=[pltpu.VMEM((4, 32, 256), F32)],
    )(*v)
    sums = a2a(sums, ("y", "x"))
    own = call(chunk_kernel, [VMEM], sds((4, 32, 256)))(sums)
    other = swap(own)
    v, own = lax.optimization_barrier((v, own))
    border = call(border_kernel, [VMEM] * 4, sds((2, 64, 256)))(*v)
    diag = call(
        finish_kernel,
        [VMEM, VMEM, VMEM, VMEM],
        sds((2, 256, 256)),
        scratch=[pltpu.VMEM((8, 32, 256), F32)],
    )(own, other, mask, terms)
    return border, diag


def solution(mesh):
    grid = Mesh(mesh.devices.reshape(4, 2, 4, 4), ALL)
    placed = (P(ROW, COL), P(), P(None, ROW, None), P(), P())
    return jax.shard_map(
        body,
        mesh=grid,
        in_specs=placed,
        out_specs=(P(None, ALL, None), P()),
        check_vma=False,
    )
```
